128 devices in a mesh: rep: 4 (over y_lo, core), fsdp: 32 (over x, y_hi, z).
Axes of the slice: x: 4, y: 4 (y_hi: 2, y_lo: 2; y = y_hi * 2 + y_lo), z: 4, core: 2. Of those that a mesh axis runs over, the one named last changes fastest.
Arguments:
- features: bfloat16 [4, 12288, 896], P('rep', 'fsdp'), may hold values from -6 to 6
- cotangent: bfloat16 [4, 12288, 4864], P('rep', 'fsdp'), may hold values from -6 to 6
- gate_weight: bfloat16 [4, 4864, 896], P('rep', 'fsdp'), may hold values from -6 to 6
- up_weight: bfloat16 [4, 4864, 896], P('rep', 'fsdp'), may hold values from -6 to 6
- gate_moment: bfloat16 [4, 4864, 896], P('rep', 'fsdp'), may hold values from -6 to 6
- up_moment: bfloat16 [4, 4864, 896], P('rep', 'fsdp'), may hold values from -6 to 6
- step_index: int32 [], replicated, may hold values from 0 to 999
Outputs:
- new_gate: bfloat16 [4, 4864, 896], P('rep', 'fsdp')
- new_up: bfloat16 [4, 4864, 896], P('rep', 'fsdp')
- new_gate_moment: bfloat16 [4, 4864, 896], P('rep', 'fsdp')
- new_up_moment: bfloat16 [4, 4864, 896], P('rep', 'fsdp')
The draws below stay inside these ranges and needn't reach their ends.
All inputs are finite; a program needn't handle non-finite values.
Results may differ from the reference program's by a relative error of at most 0.03.
Values may be sent and summed in bfloat16 or wider, within the bound.
A program may use at most 128 MiB of HBM per device.

```python
import jax
import jax.numpy as jnp
from jax import lax

D = 896
FF = 4864
TOK_DEV = 384
TOKENS = 12288
N_REP = 4
N_FSDP = 32


def spiked(values, key, source, target, blocks, factor):
    owner, partner = [(jnp.arange(values.shape[position]) // (values.shape[position] // blocks)).reshape([-1 if axis == position else 1 for axis in range(values.ndim)]) for position in (source, target)]
    chosen = jax.random.permutation(key, blocks)[partner]
    strong = (owner == chosen) | (owner == (partner + blocks // 2) % blocks)
    return jnp.where(strong, factor * values, values)


def level_of(rng, dims, pieces, least, top_value):
    level = 1.0
    for dim, blocks in pieces:
        heights = jax.random.uniform(jax.random.fold_in(jax.random.fold_in(rng, 6), dim), (blocks,), jnp.float32, least / len(pieces), top_value / len(pieces))
        level = level * jnp.repeat(jnp.exp(heights), dims[dim] // blocks).reshape((-1,) + (1,) * (len(dims) - 1 - dim))
    return level


def centred(stream_key, dims, spread, limit, shards=(), kind=jnp.bfloat16):
    result = jax.random.normal(stream_key, dims, jnp.float32) * spread
    if len(shards) > 0:
        result = level_of(stream_key, dims, shards, -0.22, 0.18) * result
    return jnp.clip(result, min=-limit, max=limit).astype(kind)


def bell_draw_with(key, shape, spread, most, pieces, heavy, kind=jnp.bfloat16):
    entries = spread * jax.random.normal(key, shape, jnp.float32)
    if pieces:
        entries = entries * level_of(key, shape, pieces, -0.22, 0.18)
    return jnp.clip(spiked(entries, jax.random.fold_in(key, 3), *heavy), -most, most).astype(kind)


def setup_inputs(seed: int = 0) -> dict:
    seeds = jax.random.split(jax.random.key(seed), 8)
    features = centred(seeds[0], (N_REP, TOKENS, D), 1.0, 6.0, ((0, 4), (1, 32)))
    cotangent = bell_draw_with(seeds[1], (N_REP, TOKENS, FF), (2 * (D / TOKENS) ** 0.5), 6.0, ((0, 4), (1, 32)), (1, 2, 32, 2.75))
    gate_weight = centred(seeds[2], (N_REP, FF, D), 1.0, 6.0, ((0, 4), (1, 32)))
    up_weight = centred(seeds[3], (N_REP, FF, D), 1.0, 6.0, ((0, 4), (1, 32)))
    gate_moment = centred(seeds[4], (N_REP, FF, D), 1.0, 6.0, ((0, 4), (1, 32)))
    up_moment = centred(seeds[5], (N_REP, FF, D), 1.0, 6.0, ((0, 4), (1, 32)))
    step_index = jax.random.randint(seeds[6], (), 0, 1000).astype(jnp.int32)
    return {"features": features, "cotangent": cotangent, "gate_weight": gate_weight, "up_weight": up_weight, "gate_moment": gate_moment, "up_moment": up_moment, "step_index": step_index}


moment_decay = 0.9
step_rate = 0.5


def derivatives(gate, upward, tangent, factor):
    sigma = jax.nn.sigmoid(gate)
    gate_diff = (factor * tangent * upward * sigma * (1.0 + gate * (1.0 - sigma))).astype(jnp.bfloat16)
    upward_diff = (factor * tangent * gate * sigma).astype(jnp.bfloat16)
    return gate_diff, upward_diff


def replica_step(features, tangent, gate_weight, up_weight, gate_moment, up_moment):
    factor = D ** -0.5
    gate = jnp.dot(features, gate_weight.T, preferred_element_type=jnp.float32) * factor
    upward = jnp.dot(features, up_weight.T, preferred_element_type=jnp.float32) * factor
    gate_diff, upward_diff = derivatives(gate, upward, tangent.astype(jnp.float32), factor)

    def add_block(totals, index):
        start = (index * TOK_DEV).astype(jnp.int32)
        block_feat = lax.dynamic_slice_in_dim(features, start, TOK_DEV, 0)
        block_gate = lax.dynamic_slice_in_dim(gate_diff, start, TOK_DEV, 0)
        block_up = lax.dynamic_slice_in_dim(upward_diff, start, TOK_DEV, 0)
        term_gate = jnp.dot(block_gate.T, block_feat, preferred_element_type=jnp.float32)
        term_up = jnp.dot(block_up.T, block_feat, preferred_element_type=jnp.float32)
        rounded = lax.optimization_barrier((term_gate.astype(jnp.bfloat16), term_up.astype(jnp.bfloat16)))
        return (totals[0] + rounded[0].astype(jnp.float32), totals[1] + rounded[1].astype(jnp.float32)), None

    zeros = jnp.zeros((FF, D), jnp.float32)
    (grad_gate, grad_up), _ = lax.scan(add_block, (zeros, zeros), jnp.arange(N_FSDP, dtype=jnp.int32))
    moment_gate = (moment_decay * gate_moment.astype(jnp.float32) + grad_gate).astype(jnp.bfloat16)
    moment_up = (moment_decay * up_moment.astype(jnp.float32) + grad_up).astype(jnp.bfloat16)
    stepped_gate = (gate_weight.astype(jnp.float32) - step_rate * moment_gate.astype(jnp.float32)).astype(jnp.bfloat16)
    stepped_up = (up_weight.astype(jnp.float32) - step_rate * moment_up.astype(jnp.float32)).astype(jnp.bfloat16)
    return stepped_gate, stepped_up, moment_gate, moment_up


def reference(features, cotangent, gate_weight, up_weight, gate_moment, up_moment, step_index):
    results = [replica_step(features[index], cotangent[index], gate_weight[index], up_weight[index], gate_moment[index], up_moment[index]) for index in range(N_REP)]
    stepped_gate = jnp.stack([item[0] for item in results])
    stepped_up = jnp.stack([item[1] for item in results])
    moment_gate = jnp.stack([item[2] for item in results])
    moment_up = jnp.stack([item[3] for item in results])
    nbits = N_REP.bit_length() - 1
    which_bit = (step_index % nbits).astype(jnp.int32)
    partners = jnp.bitwise_xor(jnp.arange(N_REP, dtype=jnp.int32), jnp.left_shift(jnp.int32(1), which_bit))
    new_gate = ((stepped_gate.astype(jnp.float32) + stepped_gate[partners].astype(jnp.float32)) * 0.5).astype(jnp.bfloat16)
    new_up = ((stepped_up.astype(jnp.float32) + stepped_up[partners].astype(jnp.float32)) * 0.5).astype(jnp.bfloat16)
    return new_gate, new_up, moment_gate, moment_up
```

```python
import functools

import jax
import jax.numpy as jnp
from jax import lax
from jax.experimental import pallas as pl
from jax.experimental.pallas import tpu as pltpu
from jax.sharding import PartitionSpec as P

MESH = pl.DeviceIdType.MESH
F32 = jnp.float32
BF16 = jnp.bfloat16
MOMENT_DECAY = 0.9
STEP_RATE = 0.5

NX, NY, NZ = 4, 2, 4
ORDER = ((2, 0), (2, 1), (1, 1), (3, 1), (1, 0), (3, 0), (0, 1), (0, 0))
SLOT = {place: index for index, place in enumerate(ORDER)}
SLOTS = len(ORDER)
AHEAD = 2


def step_kernel(
    stride,
    feat_hbm,
    cot_hbm,
    gate_hbm,
    up_hbm,
    gmom_hbm,
    umom_hbm,
    new_gate,
    new_up,
    mom_gate,
    mom_up,
    feat,
    raw,
    turned,
    cots,
    weights,
    moments,
    grad,
    terms,
    relay,
    sums,
    crossed,
    stepped,
    other,
    local_sem,
    feat_send,
    feat_recv,
    w_send,
    w_recv,
    w_fwd,
    cot_send,
    cot_recv,
    term_send,
    relay_recv,
    sum_recv,
    cross_send,
    cross_recv,
    swap_send,
    swap_recv,
):
    tok, width = feat_hbm.shape
    rows = gate_hbm.shape[0]
    half = tok // 2
    factor = width ** (-0.5)
    rep, place = lax.axis_index("rep"), lax.axis_index("fsdp")
    x, y, z = place // (NY * NZ), lax.rem(place // NZ, NY), lax.rem(place, NZ)

    def at(dx, dy, dz):
        return (
            rep,
            lax.rem(x + dx, NX) * (NY * NZ) + lax.rem(y + dy, NY) * NZ + lax.rem(z + dz, NZ),
        )

    if stride == 1:
        mate = (rep + 1 - 2 * lax.rem(rep, 2), place)
    else:
        mate = (lax.rem(rep + 2, 4), place)
    across = at(0, 1, 0)
    along_x = {dx: at(dx, 0, 0) for dx in (1, 2, 3)}
    along_z = {dz: at(0, 0, dz) for dz in (1, 3)}

    def copy(src, dst, send, recv, target):
        return pltpu.make_async_remote_copy(
            src_ref=src, dst_ref=dst, send_sem=send, recv_sem=recv, device_id=target, device_id_type=MESH
        )

    barrier = pltpu.get_barrier_semaphore()
    greeted = [mate, across, *along_x.values(), *along_z.values()]
    for target in greeted:
        pl.semaphore_signal(barrier, inc=1, device_id=target, device_id_type=MESH)
    pl.semaphore_wait(barrier, len(greeted))

    own = SLOT[0, 0]
    local = [
        pltpu.make_async_copy(cot_hbm, raw, local_sem.at[0]),
        pltpu.make_async_copy(feat_hbm, feat.at[pl.ds(0, tok)], local_sem.at[1]),
        pltpu.make_async_copy(gate_hbm, weights.at[own, 0], local_sem.at[2]),
        pltpu.make_async_copy(up_hbm, weights.at[own, 1], local_sem.at[3]),
        pltpu.make_async_copy(gmom_hbm, moments.at[0], local_sem.at[4]),
        pltpu.make_async_copy(umom_hbm, moments.at[1], local_sem.at[5]),
    ]
    for item in local:
        item.start()

    mine = (gate_hbm, up_hbm)
    partner = SLOT[0, 1]

    def w_cross(kind):
        return copy(mine[kind], weights.at[partner, kind], w_send.at[0, kind], w_recv.at[partner, kind], across)

    def w_next(dz, dy, kind):
        source = mine[kind] if dy == 0 else weights.at[partner, kind]
        slot = SLOT[NZ - dz, dy]
        return copy(
            source, weights.at[slot, kind], w_send.at[1 + dz // 2 + 2 * dy, kind], w_recv.at[slot, kind], along_z[dz]
        )

    def w_on(dz, dy):
        kind = 0 if dz == 1 else 1
        slot = SLOT[2, dy]
        return copy(
            weights.at[SLOT[NZ - dz, dy], kind], weights.at[slot, kind], w_fwd.at[dy, kind], w_recv.at[slot, kind],
            along_z[dz],
        )

    def f_next(dx, part):
        there = feat.at[pl.ds((NX - dx) * tok + part * half, half)]
        source = feat_hbm.at[pl.ds(part * half, half)]
        return copy(source, there, feat_send.at[dx // 2, part], feat_recv.at[dx // 2, part], along_x[dx])

    def f_on(dx):
        part = 0 if dx == 1 else 1
        source = feat.at[pl.ds((NX - dx) * tok + part * half, half)]
        there = feat.at[pl.ds(2 * tok + part * half, half)]
        return copy(source, there, feat_send.at[2, part], feat_recv.at[2, part], along_x[dx])

    def slot_of(index, x_there):
        dz = jnp.where(index < 2, 2, jnp.where(index < 6, jnp.where(lax.rem(index, 2) == 0, 1, 3), 0))
        dy = jnp.where((index == 0) | (index == 4) | (index == 5) | (index == 7), 0, 1)
        return lax.rem(x_there, NX) * (NY * NZ) + lax.rem(y + dy, NY) * NZ + lax.rem(z + dz, NZ)

    def c_send(index, dx):
        source = turned.at[slot_of(index, x + dx)]
        there = NX - dx - 1
        return copy(
            source, cots.at[there, index], cot_send.at[there, index], cot_recv.at[there, index], along_x[dx]
        )

    for kind in (0, 1):
        w_cross(kind).start()
    for kind in (0, 1):
        w_next(1, 0, kind).start()
        w_next(3, 0, 1 - kind).start()
        f_next(1, kind).start()
        f_next(3, 1 - kind).start()

    local[0].wait()
    group = 16 * rows

    def turn(g, carry):
        part = raw[:, pl.ds(pl.multiple_of(g * group, 128), group)].astype(F32).T
        for s in range(16):
            turned[g * 16 + s] = part[s * rows : (s + 1) * rows].astype(BF16)
        return carry

    lax.fori_loop(0, raw.shape[1] // group, turn, 0)

    for dz in (1, 3):
        kind = 0 if dz == 1 else 1
        w_next(dz, 0, kind).wait_recv()
        w_on(dz, 0).start()
    for dx in (1, 3):
        f_next(dx, 0 if dx == 1 else 1).wait_recv()
        f_on(dx).start()
    for kind in (0, 1):
        w_cross(kind).wait_recv()
        for dz in (1, 3):
            w_next(dz, 1, kind).start()
    for index in range(AHEAD):
        for dx in (1, 3, 2):
            c_send(index, dx).start()
    for dz in (1, 3):
        kind = 0 if dz == 1 else 1
        w_next(dz, 1, kind).wait_recv()
        w_on(dz, 1).start()
    for item in local[1:]:
        item.wait()
    f_next(1, 1).wait_recv()
    f_next(3, 0).wait_recv()
    f_on(1).wait_recv()
    f_on(3).wait_recv()

    def t_send(slot, kind):
        dz, dy = ORDER[slot]
        way = {(2, 0): 1, (2, 1): 3}.get((dz, kind), dz)
        if dz == 2:
            there, recv = relay.at[dy, kind], relay_recv.at[dy, kind]
        else:
            side = 0 if dz == 1 else 1
            there, recv = sums.at[side, dy, kind], sum_recv.at[side, dy, kind]
        return copy(terms.at[slot, kind], there, term_send.at[slot, kind], recv, along_z[way])

    def cross(kind):
        return copy(terms.at[partner, kind], crossed.at[kind], cross_send.at[kind], cross_recv.at[kind], across)

    def total(dy, kind):
        for side in (0, 1):
            t_send(SLOT[1 if side == 0 else 3, dy], kind).wait_recv()
        own_term = grad[pl.ds(kind * rows, rows)]
        return own_term + sums[0, dy, kind].astype(F32) + sums[1, dy, kind].astype(F32)

    def chunk(index, carry):
        for slot, (dz, dy) in enumerate(ORDER):
            if dz == 2:
                arrivals = [w_on(1, dy), w_on(3, dy)]
            elif dz == 1:
                arrivals = [w_next(3, dy, 0)]
            elif dz == 3:
                arrivals = [w_next(1, dy, 1)]
            else:
                arrivals = []
            if arrivals:

                @pl.when(index == slot)
                def _():
                    for item in arrivals:
                        item.wait_recv()

        for dx in (1, 3, 2):
            c_send(index, dx).wait_recv()

        @pl.when(index + AHEAD < SLOTS)
        def _():
            for dx in (1, 3, 2):
                c_send(index + AHEAD, dx).start()

        both = jnp.concatenate([weights[index, 0].astype(F32), weights[index, 1].astype(F32)], 0).astype(BF16)
        made = lax.dot_general(both, feat[...], (((1,), (1,)), ((), ())), preferred_element_type=F32) * factor
        gate, upward = made[:rows], made[rows:]
        tangent = jnp.concatenate(
            [turned[slot_of(index, x)].astype(F32)] + [cots[dx, index].astype(F32) for dx in range(NX - 1)], 1
        )
        sigma = jax.nn.sigmoid(gate)
        scaled = factor * tangent * sigma
        gate_diff = scaled * upward * (1.0 + gate * (1.0 - sigma))
        upward_diff = scaled * gate
        diffs = jnp.concatenate([gate_diff, upward_diff], 0).astype(BF16)
        grad[...] = jnp.dot(diffs, feat[...], preferred_element_type=F32)

        for slot, (dz, dy) in enumerate(ORDER[:-1]):

            @pl.when(index == slot)
            def _():
                for kind in (0, 1):
                    if dz == 0:
                        terms[slot, kind] = total(dy, kind).astype(BF16)
                        cross(kind).start()
                    else:
                        term = grad[pl.ds(kind * rows, rows)]
                        if (dz, kind) in ((1, 0), (3, 1)):
                            t_send(SLOT[2, dy], kind).wait_recv()
                            term = term + relay[dy, kind].astype(F32)
                        terms[slot, kind] = term.astype(BF16)
                        t_send(slot, kind).start()

        return carry

    lax.fori_loop(0, SLOTS, chunk, 0)

    def swap(kind):
        return copy(stepped.at[kind], other.at[kind], swap_send.at[kind], swap_recv.at[kind], mate)

    for kind, out in ((0, mom_gate), (1, mom_up)):
        value = total(0, kind)
        cross(kind).wait_recv()
        value = value + crossed[kind].astype(F32)
        moment = (MOMENT_DECAY * moments[kind].astype(F32) + value).astype(BF16)
        out[...] = moment
        stepped[kind] = (weights[own, kind].astype(F32) - STEP_RATE * moment.astype(F32)).astype(BF16)
        swap(kind).start()
    for kind, out in ((0, new_gate), (1, new_up)):
        swap(kind).wait_recv()
        out[...] = ((stepped[kind].astype(F32) + other[kind].astype(F32)) * 0.5).astype(BF16)

    for kind in (0, 1):
        w_cross(kind).wait_send()
        cross(kind).wait_send()
        swap(kind).wait_send()
        for dz in (1, 3):
            for dy in (0, 1):
                w_next(dz, dy, kind).wait_send()
        for dx in (1, 3):
            f_next(dx, kind).wait_send()
        for slot, (dz, dy) in enumerate(ORDER):
            if dz:
                t_send(slot, kind).wait_send()
    for dz in (1, 3):
        for dy in (0, 1):
            w_on(dz, dy).wait_send()
    for dx in (1, 3):
        f_on(dx).wait_send()

    def drain(index, carry):
        for dx in (1, 3, 2):
            c_send(index, dx).wait_send()
        return carry

    lax.fori_loop(0, SLOTS, drain, 0)


def step_call(stride, features, cotangent, gate_weight, up_weight, gate_moment, up_moment):
    tok, width = features.shape
    rows = gate_weight.shape[0]
    hidden = cotangent.shape[1]
    dma = pltpu.SemaphoreType.DMA
    out = jax.ShapeDtypeStruct((rows, width), BF16)
    return pl.pallas_call(
        functools.partial(step_kernel, stride),
        out_shape=(out,) * 4,
        in_specs=[pl.BlockSpec(memory_space=pl.ANY)] * 6,
        out_specs=(pl.BlockSpec(memory_space=pltpu.VMEM),) * 4,
        scratch_shapes=[
            pltpu.VMEM((NX * tok, width), BF16),
            pltpu.VMEM((tok, hidden), BF16),
            pltpu.VMEM((hidden // rows, rows, tok), BF16),
            pltpu.VMEM((NX - 1, SLOTS, rows, tok), BF16),
            pltpu.VMEM((SLOTS, 2, rows, width), BF16),
            pltpu.VMEM((2, rows, width), BF16),
            pltpu.VMEM((2 * rows, width), F32),
            pltpu.VMEM((SLOTS - 1, 2, rows, width), BF16),
            pltpu.VMEM((2, 2, rows, width), BF16),
            pltpu.VMEM((2, 2, 2, rows, width), BF16),
            pltpu.VMEM((2, rows, width), BF16),
            pltpu.VMEM((2, rows, width), BF16),
            pltpu.VMEM((2, rows, width), BF16),
            dma((6,)),
            dma((3, 2)),
            dma((3, 2)),
            dma((5, 2)),
            dma((SLOTS, 2)),
            dma((2, 2)),
            dma((NX - 1, SLOTS)),
            dma((NX - 1, SLOTS)),
            dma((SLOTS - 1, 2)),
            dma((2, 2)),
            dma((2, 2, 2)),
            dma((2,)),
            dma((2,)),
            dma((2,)),
            dma((2,)),
        ],
        compiler_params=pltpu.CompilerParams(
            collective_id=stride - 1, has_side_effects=True, vmem_limit_bytes=56 * 2**20
        ),
        cost_estimate=pl.CostEstimate(
            flops=8 * tok * hidden * width, bytes_accessed=2 * tok * (hidden + width), transcendentals=tok * hidden
        ),
        name=f"step_stride_{stride}",
    )(features, cotangent, gate_weight, up_weight, gate_moment, up_moment)


def body(features, cotangent, gate_weight, up_weight, gate_moment, up_moment, step_index):
    arrays = [a[0] for a in (features, cotangent, gate_weight, up_weight, gate_moment, up_moment)]
    nbits = lax.axis_size("rep").bit_length() - 1
    branches = [functools.partial(step_call, 2**bit) for bit in range(nbits)]
    results = lax.switch(step_index % nbits, branches, *arrays)
    return tuple(result[None] for result in results)


def solution(mesh):
    split = P("rep", "fsdp", None)
    return jax.shard_map(
        body, mesh=mesh, in_specs=(split,) * 6 + (P(),), out_specs=(split,) * 4, check_vma=False
    )
```

```python
import functools

import jax
import jax.numpy as jnp
from jax import lax
from jax.experimental import pallas as pl
from jax.experimental.pallas import tpu as pltpu
from jax.sharding import PartitionSpec as P

MESH = pl.DeviceIdType.MESH
F32 = jnp.float32
BF16 = jnp.bfloat16
MOMENT_DECAY = 0.9
STEP_RATE = 0.5

NX, NY, NZ = 4, 2, 4
FAR, FAR_MATE, NEXT, NEXT_MATE, BACK, BACK_MATE, OWN, OWN_MATE = (2, 0), (2, 1), (1, 0), (1, 1), (3, 0), (3, 1), (0, 0), (0, 1)
SLOT = {place: i for i, place in enumerate((FAR_MATE, NEXT_MATE, BACK_MATE, FAR, OWN_MATE, NEXT, BACK, OWN))}
CHUNKS = (
    ((FAR_MATE, 0), (FAR_MATE, 1)),
    ((NEXT_MATE, 0), (BACK_MATE, 0)),
    ((NEXT_MATE, 1), (BACK_MATE, 1)),
    ((FAR, 0), (FAR, 1)),
    ((OWN_MATE, 0), (OWN_MATE, 1)),
    ((NEXT, 0), (BACK, 0)),
    ((NEXT, 1), (BACK, 1)),
    ((OWN, 0),),
    ((OWN, 1),),
)
PIECES = tuple(piece for chunk in CHUNKS for piece in chunk)
AHEAD = 6
SEMS = 96


def sizes(rows):
    first = (rows // 2 + 15) // 16 * 16
    return first, rows - first


def step_kernel(stride, feat_hbm, cot_hbm, gate_hbm, up_hbm, gmom_hbm, umom_hbm, *refs):
    new_gate, new_up, mom_gate, mom_up = refs[:4]
    (feat, raw, weights, moments, grad, send_sems, recv_sems, local_sem) = refs[4:12]
    turned, cots, terms, far, relay, sums, crossed, stepped, other = (refs[i : i + 2] for i in range(12, 30, 2))
    tok, width = feat_hbm.shape
    rows = gate_hbm.shape[0]
    size = sizes(rows)
    span = (pl.ds(0, size[0]), pl.ds(size[0], size[1]))
    half = tok // 2
    factor = width ** (-0.5)
    rep, place = lax.axis_index("rep"), lax.axis_index("fsdp")
    x, y, z = place // (NY * NZ), lax.rem(place // NZ, NY), lax.rem(place, NZ)

    def index_of(dx, dy, dz):
        return lax.rem(x + dx, NX) * (NY * NZ) + lax.rem(y + dy, NY) * NZ + lax.rem(z + dz, NZ)

    mate = (rep + 1 - 2 * lax.rem(rep, 2), place) if stride == 1 else (lax.rem(rep + 2, 4), place)
    across = (rep, index_of(0, 1, 0))
    along_x = {dx: (rep, index_of(dx, 0, 0)) for dx in (1, 2, 3)}
    along_z = {dz: (rep, index_of(0, 0, dz)) for dz in (1, 3)}
    sent = {}

    def send(name, src, dst, target):
        number = len(sent)
        sent[name] = pltpu.make_async_remote_copy(
            src_ref=src,
            dst_ref=dst,
            send_sem=send_sems.at[number],
            recv_sem=recv_sems.at[number],
            device_id=target,
            device_id_type=MESH,
        )
        sent[name].start()

    def arrive(*name):
        sent[name].wait_recv()

    barrier = pltpu.get_barrier_semaphore()
    greeted = [mate, across, *along_x.values(), *along_z.values()]
    for target in greeted:
        pl.semaphore_signal(barrier, inc=1, device_id=target, device_id_type=MESH)
    pl.semaphore_wait(barrier, len(greeted))

    own_weights = (gate_hbm, up_hbm)

    def send_features(dx, part):
        there = feat.at[pl.ds((NX - dx) * tok + part * half, half)]
        send(("feat", dx, part), feat_hbm.at[pl.ds(part * half, half)], there, along_x[dx])

    turn_copy = pltpu.make_async_copy(cot_hbm, raw, local_sem.at[0])
    turn_copy.start()
    for kind in (0, 1):
        for dz, what in ((1, kind), (3, 1 - kind)):
            send(("w", dz, what), own_weights[what], weights.at[SLOT[NZ - dz, 0], what], along_z[dz])
        send_features(1, kind)
        send_features(3, 1 - kind)
        send(("w", "y", kind), own_weights[kind], weights.at[SLOT[OWN_MATE], kind], across)
    local = [
        pltpu.make_async_copy(feat_hbm, feat.at[pl.ds(0, tok)], local_sem.at[1]),
        pltpu.make_async_copy(gate_hbm, weights.at[SLOT[OWN], 0], local_sem.at[2]),
        pltpu.make_async_copy(up_hbm, weights.at[SLOT[OWN], 1], local_sem.at[3]),
        pltpu.make_async_copy(gmom_hbm, moments.at[0], local_sem.at[4]),
        pltpu.make_async_copy(umom_hbm, moments.at[1], local_sem.at[5]),
    ]
    for item in local:
        item.start()

    turn_copy.wait()
    group = 16 * rows

    def turn(g, carry):
        flat = raw[:, pl.ds(pl.multiple_of(g * group, 128), group)].astype(F32).T
        for s in range(16):
            turned[0][g * 16 + s] = flat[s * rows : s * rows + size[0]].astype(BF16)
            turned[1][g * 16 + s] = flat[s * rows + size[0] : (s + 1) * rows].astype(BF16)
        return carry

    lax.fori_loop(0, raw.shape[1] // group, turn, 0)

    for dz, kind in ((1, 0), (3, 1)):
        arrive("w", dz, kind)
        send(("w on", kind), weights.at[SLOT[NZ - dz, 0], kind], weights.at[SLOT[FAR], kind], along_z[dz])
    for dx, part in ((1, 0), (3, 1)):
        arrive("feat", dx, part)
        source = feat.at[pl.ds((NX - dx) * tok + part * half, half)]
        send(("feat on", part), source, feat.at[pl.ds(2 * tok + part * half, half)], along_x[dx])
    for kind in (0, 1):
        arrive("w", "y", kind)
        for dz in (1, 3):
            source = weights.at[SLOT[OWN_MATE], kind]
            send(("w mate", dz, kind), source, weights.at[SLOT[NZ - dz, 1], kind], along_z[dz])

    started = [0]

    def send_cots(upto):
        for number in range(started[0], min(upto, len(PIECES))):
            (dz, dy), part = PIECES[number]
            for dx in (1, 3, 2):
                source = turned[part].at[index_of(dx, dy, dz)]
                there = cots[part].at[NX - dx - 1, SLOT[dz, dy]]
                send(("cot", dx, number), source, there, along_x[dx])
        started[0] = max(started[0], upto)

    send_cots(AHEAD)
    for kind in (0, 1):
        arrive("w on", kind)
        send(("w far", kind), weights.at[SLOT[FAR], kind], weights.at[SLOT[FAR_MATE], kind], across)
    for item in local:
        item.wait()
    arrive("feat", 1, 1)
    arrive("feat", 3, 0)
    arrive("feat on", 0)
    arrive("feat on", 1)

    def products(pieces):
        operand, diffs, top = [], [], 0
        for slot, part in pieces:
            operand += [weights[SLOT[slot], kind, span[part]].astype(F32) for kind in (0, 1)]
        operand = jnp.concatenate(operand, 0).astype(BF16)
        made = lax.dot_general(operand, feat[...], (((1,), (1,)), ((), ())), preferred_element_type=F32) * factor
        for (dz, dy), part in pieces:
            n = size[part]
            gate, upward = made[top : top + n], made[top + n : top + 2 * n]
            top += 2 * n
            blocks = [turned[part][index_of(0, dy, dz)]] + [cots[part][dx, SLOT[dz, dy]] for dx in range(NX - 1)]
            tangent = jnp.concatenate([block.astype(F32) for block in blocks], 1)
            sigma = jax.nn.sigmoid(gate)
            scaled = factor * tangent * sigma
            diffs += [scaled * upward * (1.0 + gate * (1.0 - sigma)), scaled * gate]
        diffs = jnp.concatenate(diffs, 0).astype(BF16)
        grad[pl.ds(0, top)] = jnp.dot(diffs, feat[...], preferred_element_type=F32)

    def sides(dy, part):
        arrive("term", 1, dy, part)
        arrive("term", 3, dy, part)
        return sums[part][0, dy].astype(F32) + sums[part][1, dy].astype(F32)

    def finish(part):
        value = grad[pl.ds(0, 2 * size[part])] + sides(0, part)
        arrive("cross", part)
        value = value + crossed[part][...].astype(F32)
        n = size[part]
        for kind, out in ((0, mom_gate), (1, mom_up)):
            here = pl.ds(kind * n, n)
            moment = MOMENT_DECAY * moments[kind, span[part]].astype(F32) + value[kind * n : (kind + 1) * n]
            moment = moment.astype(BF16)
            out[span[part]] = moment
            weight = weights[SLOT[OWN], kind, span[part]].astype(F32)
            stepped[part][here] = (weight - STEP_RATE * moment.astype(F32)).astype(BF16)
        send(("swap", part), stepped[part], other[part], mate)

    for order, pieces in enumerate(CHUNKS):
        for slot, part in pieces:
            dz, dy = slot
            if slot == FAR_MATE and part == 0:
                arrive("w far", 0)
                arrive("w far", 1)
            if slot in (NEXT_MATE, BACK_MATE) and part == 0:
                arrive("w mate", NZ - dz, 0)
                arrive("w mate", NZ - dz, 1)
            if slot in (NEXT, BACK) and part == 0:
                arrive("w", NZ - dz, 0 if dz == 1 else 1)
            number = PIECES.index((slot, part))
            for dx in (1, 3, 2):
                arrive("cot", dx, number)
        send_cots(2 * order + 2 + AHEAD)
        products(pieces)
        top = 0
        for slot, part in pieces:
            (dz, dy), n = slot, 2 * size[part]
            here = terms[part].at[SLOT[slot]]
            if slot == OWN:
                finish(part)
                continue
            term = grad[pl.ds(top, n)]
            top += n
            if slot == FAR_MATE:
                here[...] = term.astype(BF16)
                send(("far", part), here, far[part], across)
            elif slot == FAR:
                arrive("far", part)
                here[...] = (term + far[part][...].astype(F32)).astype(BF16)
                send(("relay", part), here, relay[part], along_z[1 if part == 0 else 3])
            elif slot == OWN_MATE:
                here[...] = (term + sides(1, part)).astype(BF16)
                send(("cross", part), here, crossed[part], across)
            else:
                if dy == 0 and part == (0 if dz == 1 else 1):
                    arrive("relay", part)
                    term = term + relay[part][...].astype(F32)
                here[...] = term.astype(BF16)
                send(("term", dz, dy, part), here, sums[part].at[dz // 2, dy], along_z[dz])

    for part in (0, 1):
        arrive("swap", part)
        average = (stepped[part][...].astype(F32) + other[part][...].astype(F32)) * 0.5
        n = size[part]
        new_gate[span[part]] = average[:n].astype(BF16)
        new_up[span[part]] = average[n:].astype(BF16)

    for item in sent.values():
        item.wait_send()


def step_call(stride, features, cotangent, gate_weight, up_weight, gate_moment, up_moment):
    tok, width = features.shape
    rows = gate_weight.shape[0]
    hidden = cotangent.shape[1]
    slots = hidden // rows
    size = sizes(rows)
    dma = pltpu.SemaphoreType.DMA
    out = jax.ShapeDtypeStruct((rows, width), BF16)

    def parts(*lead, of=2, last=width):
        return [pltpu.VMEM((*lead, of * n, last), BF16) for n in size]

    return pl.pallas_call(
        functools.partial(step_kernel, stride),
        out_shape=(out,) * 4,
        in_specs=[pl.BlockSpec(memory_space=pl.ANY)] * 6,
        out_specs=(pl.BlockSpec(memory_space=pltpu.VMEM),) * 4,
        scratch_shapes=[
            pltpu.VMEM((NX * tok, width), BF16),
            pltpu.VMEM((tok, hidden), BF16),
            pltpu.VMEM((NY * NZ, 2, rows, width), BF16),
            pltpu.VMEM((2, rows, width), BF16),
            pltpu.VMEM((4 * size[0], width), F32),
            dma((SEMS,)),
            dma((SEMS,)),
            dma((6,)),
            *parts(slots, of=1, last=tok),
            *parts(NX - 1, NY * NZ, of=1, last=tok),
            *parts(NY * NZ - 1),
            *parts(),
            *parts(),
            *parts(2, 2),
            *parts(),
            *parts(),
            *parts(),
        ],
        compiler_params=pltpu.CompilerParams(
            collective_id=stride - 1, has_side_effects=True, vmem_limit_bytes=56 * 2**20
        ),
        cost_estimate=pl.CostEstimate(
            flops=8 * tok * hidden * width, bytes_accessed=2 * tok * (hidden + width), transcendentals=tok * hidden
        ),
        name=f"step_stride_{stride}",
    )(features, cotangent, gate_weight, up_weight, gate_moment, up_moment)


def store_kernel(*refs):
    sources, targets, sem = refs[:4], refs[4:8], refs[8]
    copies = [pltpu.make_async_copy(s, t, sem.at[i]) for i, (s, t) in enumerate(zip(sources, targets))]
    for item in copies:
        item.start()
    for item in copies:
        item.wait()


def store(arrays):
    return pl.pallas_call(
        store_kernel,
        out_shape=tuple(jax.ShapeDtypeStruct(a.shape, a.dtype) for a in arrays),
        in_specs=[pl.BlockSpec(memory_space=pltpu.VMEM)] * 4,
        out_specs=(pl.BlockSpec(memory_space=pl.ANY),) * 4,
        scratch_shapes=[pltpu.SemaphoreType.DMA((4,))],
        name="store",
    )(*arrays)


def body(features, cotangent, gate_weight, up_weight, gate_moment, up_moment, step_index):
    arrays = [a[0] for a in (features, cotangent, gate_weight, up_weight, gate_moment, up_moment)]
    nbits = lax.axis_size("rep").bit_length() - 1
    branches = [functools.partial(step_call, 2**bit) for bit in range(nbits)]
    results = store(lax.switch(step_index % nbits, branches, *arrays))
    return tuple(result[None] for result in results)


def solution(mesh):
    split = P("rep", "fsdp", None)
    return jax.shard_map(
        body, mesh=mesh, in_specs=(split,) * 6 + (P(),), out_specs=(split,) * 4, check_vma=False
    )
```

```python
import functools

import jax
import jax.numpy as jnp
from jax import lax
from jax.experimental import pallas as pl
from jax.experimental.pallas import tpu as pltpu
from jax.sharding import PartitionSpec as P

MESH = pl.DeviceIdType.MESH
F32 = jnp.float32
BF16 = jnp.bfloat16
MOMENT_DECAY = 0.9
STEP_RATE = 0.5

NX, NY, NZ = 4, 2, 4
PLACES = {
    "far": (2, 0),
    "far mate": (2, 1),
    "next": (1, 0),
    "next mate": (1, 1),
    "back": (3, 0),
    "back mate": (3, 1),
    "own": (0, 0),
    "own mate": (0, 1),
}
FAR, FAR_MATE, NEXT, NEXT_MATE, BACK, BACK_MATE, OWN, OWN_MATE = PLACES.values()
SLOT = {place: i for i, place in enumerate((FAR_MATE, NEXT_MATE, BACK_MATE, FAR, OWN_MATE, NEXT, BACK, OWN))}
ORDERS = {
    1: (
        ("back mate", 1), ("next mate", 0), ("far mate", 0), ("back mate", 0), ("next mate", 1), ("far mate", 1), ("far", 0), ("back", 0),
        ("far", 1), ("own mate", 1), ("next", 0), ("own mate", 0), ("back", 1), ("next", 1), ("own", 0), ("own", 1),
    ),
    2: (
        ("next mate", 1), ("back", 0), ("next mate", 0), ("far mate", 0), ("back mate", 0), ("far mate", 1), ("far", 0), ("back mate", 1),
        ("own mate", 0), ("far", 1), ("next", 0), ("own mate", 1), ("next", 1), ("own", 0), ("back", 1), ("own", 1),
    ),
}
ORDERS = {stride: tuple((PLACES[name], part) for name, part in order) for stride, order in ORDERS.items()}
AHEAD = 6


def sizes(rows):
    first = (rows // 2 + 15) // 16 * 16
    return first, rows - first


def choose(values, index):
    result = values[0]
    for number, value in enumerate(values[1:], 1):
        result = jnp.where(index == number, value, result)
    return result


def step_kernel(stride, feat_hbm, cot_hbm, gate_hbm, up_hbm, gmom_hbm, umom_hbm, *refs):
    new_gate, new_up, mom_gate, mom_up = refs[:4]
    (feat, raw, weights, moments, grad, send_sems, recv_sems, local_sem) = refs[4:12]
    n_parts = len(sizes(gate_hbm.shape[0]))
    turned, cots, terms, far, relay, sums, crossed, stepped, other = (
        refs[12 + i * n_parts : 12 + (i + 1) * n_parts] for i in range(9)
    )
    pieces = ORDERS[stride]
    tok, width = feat_hbm.shape
    rows = gate_hbm.shape[0]
    size = sizes(rows)
    first = [sum(size[:part]) for part in range(n_parts)]
    span = [pl.ds(first[part], size[part]) for part in range(n_parts)]
    half = tok // 2
    factor = width ** (-0.5)
    rep, place = lax.axis_index("rep"), lax.axis_index("fsdp")
    x, y, z = place // (NY * NZ), lax.rem(place // NZ, NY), lax.rem(place, NZ)

    def index_of(dx, dy, dz):
        return lax.rem(x + dx, NX) * (NY * NZ) + lax.rem(y + dy, NY) * NZ + lax.rem(z + dz, NZ)

    mate = (rep + 1 - 2 * lax.rem(rep, 2), place) if stride == 1 else (lax.rem(rep + 2, 4), place)
    across = (rep, index_of(0, 1, 0))
    along_x = {dx: (rep, index_of(dx, 0, 0)) for dx in (1, 2, 3)}
    along_z = {dz: (rep, index_of(0, 0, dz)) for dz in (1, 3)}
    sent = {}

    def relayed(part):
        return 1 if part % 2 == 0 else 3

    def plan(name, src, dst, target):
        number = len(sent)
        sent[name] = pltpu.make_async_remote_copy(
            src_ref=src,
            dst_ref=dst,
            send_sem=send_sems.at[number],
            recv_sem=recv_sems.at[number],
            device_id=target,
            device_id_type=MESH,
        )

    def go(*name):
        sent[name].start()

    def send(name, src, dst, target):
        plan(name, src, dst, target)
        go(*name)

    arrived = set()

    def arrive(*name):
        if name not in arrived:
            arrived.add(name)
            sent[name].wait_recv()

    barrier = pltpu.get_barrier_semaphore()
    greeted = [mate, across, *along_x.values(), *along_z.values()]
    for target in greeted:
        pl.semaphore_signal(barrier, inc=1, device_id=target, device_id_type=MESH)
    pl.semaphore_wait(barrier, len(greeted))

    own_weights = (gate_hbm, up_hbm)

    def send_features(dx, part):
        there = feat.at[pl.ds((NX - dx) * tok + part * half, half)]
        send(("feat", dx, part), feat_hbm.at[pl.ds(part * half, half)], there, along_x[dx])

    turn_copy = pltpu.make_async_copy(cot_hbm, raw, local_sem.at[0])
    turn_copy.start()
    for kind in (0, 1):
        for dz, what in ((1, kind), (3, 1 - kind)):
            send(("w", dz, what), own_weights[what], weights.at[SLOT[NZ - dz, 0], what], along_z[dz])
        send_features(1, kind)
        send_features(3, 1 - kind)
        send(("w", "y", kind), own_weights[kind], weights.at[SLOT[OWN_MATE], kind], across)
    local = [
        pltpu.make_async_copy(feat_hbm, feat.at[pl.ds(0, tok)], local_sem.at[1]),
        pltpu.make_async_copy(gate_hbm, weights.at[SLOT[OWN], 0], local_sem.at[2]),
        pltpu.make_async_copy(up_hbm, weights.at[SLOT[OWN], 1], local_sem.at[3]),
        pltpu.make_async_copy(gmom_hbm, moments.at[0], local_sem.at[4]),
        pltpu.make_async_copy(umom_hbm, moments.at[1], local_sem.at[5]),
    ]
    for item in local:
        item.start()

    turn_copy.wait()
    group = 16 * rows

    def turn(g, carry):
        flat = raw[:, pl.ds(pl.multiple_of(g * group, 128), group)].astype(F32).T
        for s in range(16):
            for part in range(n_parts):
                top = s * rows + first[part]
                turned[part][g * 16 + s] = flat[top : top + size[part]].astype(BF16)
        return carry

    lax.fori_loop(0, raw.shape[1] // group, turn, 0)

    for dz, kind in ((1, 0), (3, 1)):
        arrive("w", dz, kind)
        send(("w on", kind), weights.at[SLOT[NZ - dz, 0], kind], weights.at[SLOT[FAR], kind], along_z[dz])
    for dx, part in ((1, 0), (3, 1)):
        arrive("feat", dx, part)
        source = feat.at[pl.ds((NX - dx) * tok + part * half, half)]
        send(("feat on", part), source, feat.at[pl.ds(2 * tok + part * half, half)], along_x[dx])
    for kind in (0, 1):
        arrive("w", "y", kind)
        for dz in (1, 3):
            source = weights.at[SLOT[OWN_MATE], kind]
            send(("w mate", dz, kind), source, weights.at[SLOT[NZ - dz, 1], kind], along_z[dz])

    for number, ((dz, dy), part) in enumerate(pieces):
        for dx in (1, 3, 2):
            source = turned[part].at[index_of(dx, dy, dz)]
            plan(("cot", dx, number), source, cots[part].at[NX - dx - 1, SLOT[dz, dy]], along_x[dx])
    for slot, part in pieces:
        dz, dy = slot
        here = None if slot == OWN else terms[part].at[SLOT[slot]]
        if slot == FAR_MATE:
            plan(("far", part), here, far[part], across)
        elif slot == FAR:
            plan(("relay", part), here, relay[part], along_z[relayed(part)])
        elif slot == OWN_MATE:
            plan(("cross", part), here, crossed[part], across)
        elif slot == OWN:
            plan(("swap", part), stepped[part], other[part], mate)
        else:
            plan(("term", dz, dy, part), here, sums[part].at[dz // 2, dy], along_z[dz])

    def send_cots(number):
        if number < len(pieces):
            for dx in (1, 3, 2):
                go("cot", dx, number)

    for number in range(AHEAD):
        send_cots(number)
    for kind in (0, 1):
        arrive("w on", kind)
        send(("w far", kind), weights.at[SLOT[FAR], kind], weights.at[SLOT[FAR_MATE], kind], across)
    for item in local:
        item.wait()
    arrive("feat", 1, 1)
    arrive("feat", 3, 0)
    arrive("feat on", 0)
    arrive("feat on", 1)

    def products(part, slot, own):
        n = size[part]
        both = [weights[slot, kind, span[part]].astype(F32) for kind in (0, 1)]
        both = jnp.concatenate(both, 0).astype(BF16)
        made = lax.dot_general(both, feat[...], (((1,), (1,)), ((), ())), preferred_element_type=F32) * factor
        gate, upward = made[:n], made[n:]
        blocks = [turned[part][own]] + [cots[part][dx, slot] for dx in range(NX - 1)]
        tangent = jnp.concatenate([block.astype(F32) for block in blocks], 1)
        sigma = jax.nn.sigmoid(gate)
        scaled = factor * tangent * sigma
        diffs = [scaled * upward * (1.0 + gate * (1.0 - sigma)), scaled * gate]
        diffs = jnp.concatenate(diffs, 0).astype(BF16)
        grad[pl.ds(0, 2 * n)] = jnp.dot(diffs, feat[...], preferred_element_type=F32)

    def sides(dy, part):
        arrive("term", 1, dy, part)
        arrive("term", 3, dy, part)
        return sums[part][0, dy].astype(F32) + sums[part][1, dy].astype(F32)

    def finish(part):
        n = size[part]
        value = grad[pl.ds(0, 2 * n)] + sides(0, part)
        arrive("cross", part)
        value = value + crossed[part][...].astype(F32)
        for kind, out in ((0, mom_gate), (1, mom_up)):
            moment = MOMENT_DECAY * moments[kind, span[part]].astype(F32) + value[kind * n : (kind + 1) * n]
            moment = moment.astype(BF16)
            out[span[part]] = moment
            weight = weights[SLOT[OWN], kind, span[part]].astype(F32)
            stepped[part][pl.ds(kind * n, n)] = (weight - STEP_RATE * moment.astype(F32)).astype(BF16)
        go("swap", part)

    slots = [SLOT[slot] for slot, part in pieces]
    owns = [index_of(0, dy, dz) for (dz, dy), part in pieces]

    def work(index, carry):
        for number, (slot, part) in enumerate(pieces):

            @pl.when(index == number)
            def _():
                dz, dy = slot
                for name in {
                    FAR_MATE: (("w far", 0), ("w far", 1)),
                    NEXT_MATE: (("w mate", 3, 0), ("w mate", 3, 1)),
                    BACK_MATE: (("w mate", 1, 0), ("w mate", 1, 1)),
                    NEXT: (("w", 3, 0),),
                    BACK: (("w", 1, 1),),
                }.get(slot, ()):
                    arrive(*name)
                for dx in (1, 3, 2):
                    arrive("cot", dx, number)
                send_cots(number + AHEAD)

        slot_here, own_here = choose(slots, index), choose(owns, index)
        part_here = choose([part for slot, part in pieces], index)
        for part in range(n_parts):

            @pl.when(part_here == part)
            def _():
                products(part, slot_here, own_here)

        for number, (slot, part) in enumerate(pieces):

            @pl.when(index == number)
            def _():
                dz, dy = slot
                if slot == OWN:
                    finish(part)
                    return
                term = grad[pl.ds(0, 2 * size[part])]
                name = ("term", dz, dy, part)
                if slot == FAR_MATE:
                    name = ("far", part)
                elif slot == FAR:
                    name = ("relay", part)
                    arrive("far", part)
                    term = term + far[part][...].astype(F32)
                elif slot == OWN_MATE:
                    name = ("cross", part)
                    term = term + sides(1, part)
                elif dy == 0 and dz == relayed(part):
                    arrive("relay", part)
                    term = term + relay[part][...].astype(F32)
                terms[part][SLOT[slot]] = term.astype(BF16)
                go(*name)

        return carry

    lax.fori_loop(0, len(pieces), work, 0)

    for part in range(n_parts):
        arrive("swap", part)
        average = (stepped[part][...].astype(F32) + other[part][...].astype(F32)) * 0.5
        n = size[part]
        new_gate[span[part]] = average[:n].astype(BF16)
        new_up[span[part]] = average[n:].astype(BF16)

    for item in sent.values():
        item.wait_send()


def step_call(stride, features, cotangent, gate_weight, up_weight, gate_moment, up_moment):
    tok, width = features.shape
    rows = gate_weight.shape[0]
    hidden = cotangent.shape[1]
    slots = hidden // rows
    size = sizes(rows)
    sems = 20 + 32 * len(size)
    dma = pltpu.SemaphoreType.DMA
    out = jax.ShapeDtypeStruct((rows, width), BF16)

    def parts(*lead, of=2, last=width):
        return [pltpu.VMEM((*lead, of * n, last), BF16) for n in size]

    return pl.pallas_call(
        functools.partial(step_kernel, stride),
        out_shape=(out,) * 4,
        in_specs=[pl.BlockSpec(memory_space=pl.ANY)] * 6,
        out_specs=(pl.BlockSpec(memory_space=pltpu.VMEM),) * 4,
        scratch_shapes=[
            pltpu.VMEM((NX * tok, width), BF16),
            pltpu.VMEM((tok, hidden), BF16),
            pltpu.VMEM((NY * NZ, 2, rows, width), BF16),
            pltpu.VMEM((2, rows, width), BF16),
            pltpu.VMEM((2 * max(size), width), F32),
            dma((sems,)),
            dma((sems,)),
            dma((6,)),
            *parts(slots, of=1, last=tok),
            *parts(NX - 1, NY * NZ, of=1, last=tok),
            *parts(NY * NZ - 1),
            *parts(),
            *parts(),
            *parts(2, 2),
            *parts(),
            *parts(),
            *parts(),
        ],
        compiler_params=pltpu.CompilerParams(
            collective_id=stride - 1, has_side_effects=True, vmem_limit_bytes=56 * 2**20
        ),
        cost_estimate=pl.CostEstimate(
            flops=8 * tok * hidden * width, bytes_accessed=2 * tok * (hidden + width), transcendentals=tok * hidden
        ),
        name=f"step_stride_{stride}",
    )(features, cotangent, gate_weight, up_weight, gate_moment, up_moment)


def store_kernel(*refs):
    sources, targets, sem = refs[:4], refs[4:8], refs[8]
    copies = [pltpu.make_async_copy(s, t, sem.at[i]) for i, (s, t) in enumerate(zip(sources, targets))]
    for item in copies:
        item.start()
    for item in copies:
        item.wait()


def store(arrays):
    return pl.pallas_call(
        store_kernel,
        out_shape=tuple(jax.ShapeDtypeStruct(a.shape, a.dtype) for a in arrays),
        in_specs=[pl.BlockSpec(memory_space=pltpu.VMEM)] * 4,
        out_specs=(pl.BlockSpec(memory_space=pl.ANY),) * 4,
        scratch_shapes=[pltpu.SemaphoreType.DMA((4,))],
        name="store",
    )(*arrays)


def body(features, cotangent, gate_weight, up_weight, gate_moment, up_moment, step_index):
    arrays = [a[0] for a in (features, cotangent, gate_weight, up_weight, gate_moment, up_moment)]
    nbits = lax.axis_size("rep").bit_length() - 1
    branches = [functools.partial(step_call, 2**bit) for bit in range(nbits)]
    results = store(lax.switch(lax.rem(step_index, nbits), branches, *arrays))
    return tuple(result[None] for result in results)


def solution(mesh):
    split = P("rep", "fsdp", None)
    return jax.shard_map(
        body, mesh=mesh, in_specs=(split,) * 6 + (P(),), out_specs=(split,) * 4, check_vma=False
    )
```

```python
import functools

import jax
import jax.numpy as jnp
from jax import lax
from jax.experimental import pallas as pl
from jax.experimental.pallas import tpu as pltpu
from jax.sharding import PartitionSpec as P

MESH = pl.DeviceIdType.MESH
F32 = jnp.float32
BF16 = jnp.bfloat16
MOMENT_DECAY = 0.9
STEP_RATE = 0.5

NX, NY, NZ = 4, 2, 4
PLACES = {
    "far": (2, 0),
    "far mate": (2, 1),
    "next": (1, 0),
    "next mate": (1, 1),
    "back": (3, 0),
    "back mate": (3, 1),
    "own": (0, 0),
    "own mate": (0, 1),
}
FAR, FAR_MATE, NEXT, NEXT_MATE, BACK, BACK_MATE, OWN, OWN_MATE = PLACES.values()
SLOT = {place: i for i, place in enumerate((FAR_MATE, NEXT_MATE, BACK_MATE, FAR, OWN_MATE, NEXT, BACK, OWN))}
ORDERS = {
    1: (
        ("next mate", 0), ("back mate", 0), ("far mate", 0), ("back mate", 1), ("next mate", 1), ("far mate", 1), ("far", 0), ("back", 0),
        ("own mate", 0), ("next", 0), ("far", 1), ("own mate", 1), ("next", 1), ("back", 1), ("own", 0), ("own", 1),
    ),
    2: (
        ("next mate", 0), ("far mate", 0), ("back mate", 0), ("next mate", 1), ("back", 0), ("far mate", 1), ("far", 0), ("own mate", 0),
        ("back mate", 1), ("next", 0), ("far", 1), ("own mate", 1), ("own", 0), ("next", 1), ("back", 1), ("own", 1),
    ),
}
ORDERS = {stride: tuple((PLACES[name], part) for name, part in order) for stride, order in ORDERS.items()}
AHEAD = 6


def sizes(rows):
    first = rows * 96 // 152 // 16 * 16
    return first, rows - first


def choose(values, index):
    result = values[0]
    for number, value in enumerate(values[1:], 1):
        result = jnp.where(index == number, value, result)
    return result


def step_kernel(stride, feat_hbm, cot_hbm, gate_hbm, up_hbm, gmom_hbm, umom_hbm, *refs):
    new_gate, new_up, mom_gate, mom_up = refs[:4]
    (feat, raw, weights, moments, grad, send_sems, recv_sems, local_sem) = refs[4:12]
    n_parts = len(sizes(gate_hbm.shape[0]))
    turned, cots, terms, far, relay, sums, crossed, stepped, other = (
        refs[12 + i * n_parts : 12 + (i + 1) * n_parts] for i in range(9)
    )
    pieces = ORDERS[stride]
    tok, width = feat_hbm.shape
    rows = gate_hbm.shape[0]
    size = sizes(rows)
    first = [sum(size[:part]) for part in range(n_parts)]
    span = [pl.ds(first[part], size[part]) for part in range(n_parts)]
    half = tok // 2
    factor = width ** (-0.5)
    rep, place = lax.axis_index("rep"), lax.axis_index("fsdp")
    x, y, z = place // (NY * NZ), lax.rem(place // NZ, NY), lax.rem(place, NZ)

    def index_of(dx, dy, dz):
        return lax.rem(x + dx, NX) * (NY * NZ) + lax.rem(y + dy, NY) * NZ + lax.rem(z + dz, NZ)

    mate = (rep + 1 - 2 * lax.rem(rep, 2), place) if stride == 1 else (lax.rem(rep + 2, 4), place)
    across = (rep, index_of(0, 1, 0))
    along_x = {dx: (rep, index_of(dx, 0, 0)) for dx in (1, 2, 3)}
    along_z = {dz: (rep, index_of(0, 0, dz)) for dz in (1, 3)}
    sent = {}

    def relayed(part):
        return 1 if part % 2 == 0 else 3

    def plan(name, src, dst, target):
        number = len(sent)
        sent[name] = pltpu.make_async_remote_copy(
            src_ref=src,
            dst_ref=dst,
            send_sem=send_sems.at[number],
            recv_sem=recv_sems.at[number],
            device_id=target,
            device_id_type=MESH,
        )

    def go(*name):
        sent[name].start()

    def send(name, src, dst, target):
        plan(name, src, dst, target)
        go(*name)

    arrived = set()

    def arrive(*name):
        if name not in arrived:
            arrived.add(name)
            sent[name].wait_recv()

    barrier = pltpu.get_barrier_semaphore()
    greeted = [mate, across, *along_x.values(), *along_z.values()]
    for target in greeted:
        pl.semaphore_signal(barrier, inc=1, device_id=target, device_id_type=MESH)
    pl.semaphore_wait(barrier, len(greeted))

    own_weights = (gate_hbm, up_hbm)

    def send_features(dx, part):
        there = feat.at[pl.ds((NX - dx) * tok + part * half, half)]
        send(("feat", dx, part), feat_hbm.at[pl.ds(part * half, half)], there, along_x[dx])

    turn_copy = pltpu.make_async_copy(cot_hbm, raw, local_sem.at[0])
    for kind in (0, 1):
        send_features(1, kind)
        send_features(3, 1 - kind)
        for dz, what in ((1, kind), (3, 1 - kind)):
            send(("w", dz, what), own_weights[what], weights.at[SLOT[NZ - dz, 0], what], along_z[dz])
        send(("w", "y", kind), own_weights[kind], weights.at[SLOT[OWN_MATE], kind], across)
        if kind == 0:
            turn_copy.start()
    local = [
        pltpu.make_async_copy(feat_hbm, feat.at[pl.ds(0, tok)], local_sem.at[1]),
        pltpu.make_async_copy(gate_hbm, weights.at[SLOT[OWN], 0], local_sem.at[2]),
        pltpu.make_async_copy(up_hbm, weights.at[SLOT[OWN], 1], local_sem.at[3]),
        pltpu.make_async_copy(gmom_hbm, moments.at[0], local_sem.at[4]),
        pltpu.make_async_copy(umom_hbm, moments.at[1], local_sem.at[5]),
    ]
    for item in local:
        item.start()

    turn_copy.wait()
    group = 16 * rows

    def turn(g, carry):
        flat = raw[:, pl.ds(pl.multiple_of(g * group, 128), group)].astype(F32).T
        for s in range(16):
            for part in range(n_parts):
                top = s * rows + first[part]
                turned[part][g * 16 + s] = flat[top : top + size[part]].astype(BF16)
        return carry

    lax.fori_loop(0, raw.shape[1] // group, turn, 0)

    for dz, kind in ((1, 0), (3, 1)):
        arrive("w", dz, kind)
        send(("w on", kind), weights.at[SLOT[NZ - dz, 0], kind], weights.at[SLOT[FAR], kind], along_z[dz])
    for dx, part in ((1, 0), (3, 1)):
        arrive("feat", dx, part)
        source = feat.at[pl.ds((NX - dx) * tok + part * half, half)]
        send(("feat on", part), source, feat.at[pl.ds(2 * tok + part * half, half)], along_x[dx])
    for kind in (0, 1):
        arrive("w", "y", kind)
        for dz in (1, 3):
            source = weights.at[SLOT[OWN_MATE], kind]
            send(("w mate", dz, kind), source, weights.at[SLOT[NZ - dz, 1], kind], along_z[dz])

    for number, ((dz, dy), part) in enumerate(pieces):
        for dx in (1, 3, 2):
            source = turned[part].at[index_of(dx, dy, dz)]
            plan(("cot", dx, number), source, cots[part].at[NX - dx - 1, SLOT[dz, dy]], along_x[dx])
    for slot, part in pieces:
        dz, dy = slot
        here = None if slot == OWN else terms[part].at[SLOT[slot]]
        if slot == FAR_MATE:
            plan(("far", part), here, far[part], across)
        elif slot == FAR:
            plan(("relay", part), here, relay[part], along_z[relayed(part)])
        elif slot == OWN_MATE:
            plan(("cross", part), here, crossed[part], across)
        elif slot == OWN:
            plan(("swap", part), stepped[part], other[part], mate)
        else:
            plan(("term", dz, dy, part), here, sums[part].at[dz // 2, dy], along_z[dz])

    def send_cots(number):
        if number < len(pieces):
            for dx in (1, 3, 2):
                go("cot", dx, number)

    for number in range(AHEAD):
        send_cots(number)
    for kind in (0, 1):
        arrive("w on", kind)
        send(("w far", kind), weights.at[SLOT[FAR], kind], weights.at[SLOT[FAR_MATE], kind], across)
    for item in local:
        item.wait()
    arrive("feat", 1, 1)
    arrive("feat", 3, 0)
    arrive("feat on", 0)
    arrive("feat on", 1)

    def products(part, slot, own):
        n = size[part]
        both = [weights[slot, kind, span[part]].astype(F32) for kind in (0, 1)]
        both = jnp.concatenate(both, 0).astype(BF16)
        made = lax.dot_general(both, feat[...], (((1,), (1,)), ((), ())), preferred_element_type=F32) * factor
        gate, upward = made[:n], made[n:]
        blocks = [turned[part][own]] + [cots[part][dx, slot] for dx in range(NX - 1)]
        tangent = jnp.concatenate([block.astype(F32) for block in blocks], 1)
        sigma = jax.nn.sigmoid(gate)
        scaled = factor * tangent * sigma
        diffs = [scaled * upward * (1.0 + gate * (1.0 - sigma)), scaled * gate]
        diffs = jnp.concatenate(diffs, 0).astype(BF16)
        grad[pl.ds(0, 2 * n)] = jnp.dot(diffs, feat[...], preferred_element_type=F32)

    def sides(dy, part):
        arrive("term", 1, dy, part)
        arrive("term", 3, dy, part)
        return sums[part][0, dy].astype(F32) + sums[part][1, dy].astype(F32)

    def finish(part):
        n = size[part]
        value = grad[pl.ds(0, 2 * n)] + sides(0, part)
        arrive("cross", part)
        value = value + crossed[part][...].astype(F32)
        for kind, out in ((0, mom_gate), (1, mom_up)):
            moment = MOMENT_DECAY * moments[kind, span[part]].astype(F32) + value[kind * n : (kind + 1) * n]
            moment = moment.astype(BF16)
            out[span[part]] = moment
            weight = weights[SLOT[OWN], kind, span[part]].astype(F32)
            stepped[part][pl.ds(kind * n, n)] = (weight - STEP_RATE * moment.astype(F32)).astype(BF16)
        go("swap", part)

    slots = [SLOT[slot] for slot, part in pieces]
    owns = [index_of(0, dy, dz) for (dz, dy), part in pieces]

    def work(index, carry):
        for number, (slot, part) in enumerate(pieces):

            @pl.when(index == number)
            def _():
                dz, dy = slot
                for name in {
                    FAR_MATE: (("w far", 0), ("w far", 1)),
                    NEXT_MATE: (("w mate", 3, 0), ("w mate", 3, 1)),
                    BACK_MATE: (("w mate", 1, 0), ("w mate", 1, 1)),
                    NEXT: (("w", 3, 0),),
                    BACK: (("w", 1, 1),),
                }.get(slot, ()):
                    arrive(*name)
                for dx in (1, 3, 2):
                    arrive("cot", dx, number)
                send_cots(number + AHEAD)

        slot_here, own_here = choose(slots, index), choose(owns, index)
        part_here = choose([part for slot, part in pieces], index)
        for part in range(n_parts):

            @pl.when(part_here == part)
            def _():
                products(part, slot_here, own_here)

        for number, (slot, part) in enumerate(pieces):

            @pl.when(index == number)
            def _():
                dz, dy = slot
                if slot == OWN:
                    finish(part)
                    return
                term = grad[pl.ds(0, 2 * size[part])]
                name = ("term", dz, dy, part)
                if slot == FAR_MATE:
                    name = ("far", part)
                elif slot == FAR:
                    name = ("relay", part)
                    arrive("far", part)
                    term = term + far[part][...].astype(F32)
                elif slot == OWN_MATE:
                    name = ("cross", part)
                    term = term + sides(1, part)
                elif dy == 0 and dz == relayed(part):
                    arrive("relay", part)
                    term = term + relay[part][...].astype(F32)
                terms[part][SLOT[slot]] = term.astype(BF16)
                go(*name)

        return carry

    lax.fori_loop(0, len(pieces), work, 0)

    for name, item in sent.items():
        if name[0] != "swap":
            item.wait_send()
    for part in range(n_parts):
        arrive("swap", part)
        average = (stepped[part][...].astype(F32) + other[part][...].astype(F32)) * 0.5
        n = size[part]
        new_gate[span[part]] = average[:n].astype(BF16)
        new_up[span[part]] = average[n:].astype(BF16)

    for part in range(n_parts):
        sent["swap", part].wait_send()


def step_call(stride, features, cotangent, gate_weight, up_weight, gate_moment, up_moment):
    tok, width = features.shape
    rows = gate_weight.shape[0]
    hidden = cotangent.shape[1]
    slots = hidden // rows
    size = sizes(rows)
    sems = 20 + 32 * len(size)
    dma = pltpu.SemaphoreType.DMA
    out = jax.ShapeDtypeStruct((rows, width), BF16)

    def parts(*lead, of=2, last=width):
        return [pltpu.VMEM((*lead, of * n, last), BF16) for n in size]

    return pl.pallas_call(
        functools.partial(step_kernel, stride),
        out_shape=(out,) * 4,
        in_specs=[pl.BlockSpec(memory_space=pl.ANY)] * 6,
        out_specs=(pl.BlockSpec(memory_space=pltpu.VMEM),) * 4,
        scratch_shapes=[
            pltpu.VMEM((NX * tok, width), BF16),
            pltpu.VMEM((tok, hidden), BF16),
            pltpu.VMEM((NY * NZ, 2, rows, width), BF16),
            pltpu.VMEM((2, rows, width), BF16),
            pltpu.VMEM((2 * max(size), width), F32),
            dma((sems,)),
            dma((sems,)),
            dma((6,)),
            *parts(slots, of=1, last=tok),
            *parts(NX - 1, NY * NZ, of=1, last=tok),
            *parts(NY * NZ - 1),
            *parts(),
            *parts(),
            *parts(2, 2),
            *parts(),
            *parts(),
            *parts(),
        ],
        compiler_params=pltpu.CompilerParams(
            collective_id=stride - 1, has_side_effects=True, vmem_limit_bytes=56 * 2**20
        ),
        cost_estimate=pl.CostEstimate(
            flops=8 * tok * hidden * width, bytes_accessed=2 * tok * (hidden + width), transcendentals=tok * hidden
        ),
        name=f"step_stride_{stride}",
    )(features, cotangent, gate_weight, up_weight, gate_moment, up_moment)


def store_kernel(*refs):
    sources, targets, sem = refs[:4], refs[4:8], refs[8]
    copies = [pltpu.make_async_copy(s, t, sem.at[i]) for i, (s, t) in enumerate(zip(sources, targets))]
    for item in copies:
        item.start()
    for item in copies:
        item.wait()


def store(arrays):
    return pl.pallas_call(
        store_kernel,
        out_shape=tuple(jax.ShapeDtypeStruct(a.shape, a.dtype) for a in arrays),
        in_specs=[pl.BlockSpec(memory_space=pltpu.VMEM)] * 4,
        out_specs=(pl.BlockSpec(memory_space=pl.ANY),) * 4,
        scratch_shapes=[pltpu.SemaphoreType.DMA((4,))],
        name="store",
    )(*arrays)


def body(features, cotangent, gate_weight, up_weight, gate_moment, up_moment, step_index):
    arrays = [a[0] for a in (features, cotangent, gate_weight, up_weight, gate_moment, up_moment)]
    nbits = lax.axis_size("rep").bit_length() - 1
    branches = [functools.partial(step_call, 2**bit) for bit in range(nbits)]
    results = store(lax.switch(lax.rem(step_index, nbits), branches, *arrays))
    return tuple(result[None] for result in results)


def solution(mesh):
    split = P("rep", "fsdp", None)
    return jax.shard_map(
        body, mesh=mesh, in_specs=(split,) * 6 + (P(),), out_specs=(split,) * 4, check_vma=False
    )
```

```python
import functools

import jax
import jax.numpy as jnp
from jax import lax
from jax.experimental import pallas as pl
from jax.experimental.pallas import tpu as pltpu
from jax.sharding import PartitionSpec as P

MESH = pl.DeviceIdType.MESH
F32 = jnp.float32
BF16 = jnp.bfloat16
MOMENT_DECAY = 0.9
STEP_RATE = 0.5

NX, NY, NZ = 4, 2, 4
PLACES = {
    "far": (2, 0),
    "far mate": (2, 1),
    "next": (1, 0),
    "next mate": (1, 1),
    "back": (3, 0),
    "back mate": (3, 1),
    "own": (0, 0),
    "own mate": (0, 1),
}
FAR, FAR_MATE, NEXT, NEXT_MATE, BACK, BACK_MATE, OWN, OWN_MATE = PLACES.values()
SLOT = {place: i for i, place in enumerate((FAR_MATE, NEXT_MATE, BACK_MATE, FAR, OWN_MATE, NEXT, BACK, OWN))}
ORDERS = {
    1: (
        ("next mate", 0), ("back mate", 0), ("far mate", 0), ("back mate", 1), ("next mate", 1), ("far mate", 1), ("far", 0), ("back", 0),
        ("own mate", 0), ("next", 0), ("far", 1), ("own mate", 1), ("next", 1), ("back", 1), ("own", 0), ("own", 1),
    ),
    2: (
        ("next mate", 1), ("far mate", 0), ("back mate", 1), ("next mate", 0), ("far mate", 1), ("back mate", 0), ("far", 0), ("own mate", 0),
        ("back", 0), ("next", 0), ("own mate", 1), ("far", 1), ("own", 0), ("next", 1), ("back", 1), ("own", 1),
    ),
}
ORDERS = {stride: tuple((PLACES[name], part) for name, part in order) for stride, order in ORDERS.items()}
FIRST = {1: 96, 2: 80}
AHEAD = 6


def sizes(rows, stride):
    return FIRST[stride], rows - FIRST[stride]


def choose(values, index):
    result = values[0]
    for number, value in enumerate(values[1:], 1):
        result = jnp.where(index == number, value, result)
    return result


def step_kernel(stride, feat_hbm, cot_hbm, gate_hbm, up_hbm, gmom_hbm, umom_hbm, *refs):
    new_gate, new_up, mom_gate, mom_up = refs[:4]
    (feat, raw, weights, moments, grad, send_sems, recv_sems, local_sem) = refs[4:12]
    n_parts = len(sizes(gate_hbm.shape[0], stride))
    turned, cots, terms, far, relay, sums, crossed, stepped, other = (
        refs[12 + i * n_parts : 12 + (i + 1) * n_parts] for i in range(9)
    )
    pieces = ORDERS[stride]
    tok, width = feat_hbm.shape
    rows = gate_hbm.shape[0]
    size = sizes(rows, stride)
    first = [sum(size[:part]) for part in range(n_parts)]
    span = [pl.ds(first[part], size[part]) for part in range(n_parts)]
    half = tok // 2
    factor = width ** (-0.5)
    rep, place = lax.axis_index("rep"), lax.axis_index("fsdp")
    x, y, z = place // (NY * NZ), lax.rem(place // NZ, NY), lax.rem(place, NZ)

    def index_of(dx, dy, dz):
        return lax.rem(x + dx, NX) * (NY * NZ) + lax.rem(y + dy, NY) * NZ + lax.rem(z + dz, NZ)

    mate = (rep + 1 - 2 * lax.rem(rep, 2), place) if stride == 1 else (lax.rem(rep + 2, 4), place)
    across = (rep, index_of(0, 1, 0))
    along_x = {dx: (rep, index_of(dx, 0, 0)) for dx in (1, 2, 3)}
    along_z = {dz: (rep, index_of(0, 0, dz)) for dz in (1, 3)}
    sent = {}

    def relayed(part):
        return 1 if part % 2 == 0 else 3

    def plan(name, src, dst, target):
        number = len(sent)
        sent[name] = pltpu.make_async_remote_copy(
            src_ref=src,
            dst_ref=dst,
            send_sem=send_sems.at[number],
            recv_sem=recv_sems.at[number],
            device_id=target,
            device_id_type=MESH,
        )

    def go(*name):
        sent[name].start()

    def send(name, src, dst, target):
        plan(name, src, dst, target)
        go(*name)

    arrived = set()

    def arrive(*name):
        if name not in arrived:
            arrived.add(name)
            sent[name].wait_recv()

    barrier = pltpu.get_barrier_semaphore()
    greeted = [mate, across, *along_x.values(), *along_z.values()]
    for target in greeted:
        pl.semaphore_signal(barrier, inc=1, device_id=target, device_id_type=MESH)
    pl.semaphore_wait(barrier, len(greeted))

    own_weights = (gate_hbm, up_hbm)

    def send_features(dx, part):
        there = feat.at[pl.ds((NX - dx) * tok + part * half, half)]
        send(("feat", dx, part), feat_hbm.at[pl.ds(part * half, half)], there, along_x[dx])

    turn_copy = pltpu.make_async_copy(cot_hbm, raw, local_sem.at[0])
    for kind in (0, 1):
        send_features(1, kind)
        send_features(3, 1 - kind)
        for dz, what in ((1, kind), (3, 1 - kind)):
            send(("w", dz, what), own_weights[what], weights.at[SLOT[NZ - dz, 0], what], along_z[dz])
        send(("w", "y", kind), own_weights[kind], weights.at[SLOT[OWN_MATE], kind], across)
        if kind == 0:
            turn_copy.start()
    local = [
        pltpu.make_async_copy(feat_hbm, feat.at[pl.ds(0, tok)], local_sem.at[1]),
        pltpu.make_async_copy(gate_hbm, weights.at[SLOT[OWN], 0], local_sem.at[2]),
        pltpu.make_async_copy(up_hbm, weights.at[SLOT[OWN], 1], local_sem.at[3]),
        pltpu.make_async_copy(gmom_hbm, moments.at[0], local_sem.at[4]),
        pltpu.make_async_copy(umom_hbm, moments.at[1], local_sem.at[5]),
    ]
    for item in local:
        item.start()

    turn_copy.wait()
    group = 16 * rows

    def turn(g, carry):
        flat = raw[:, pl.ds(pl.multiple_of(g * group, 128), group)].astype(F32).T
        for s in range(16):
            for part in range(n_parts):
                top = s * rows + first[part]
                turned[part][g * 16 + s] = flat[top : top + size[part]].astype(BF16)
        return carry

    lax.fori_loop(0, raw.shape[1] // group, turn, 0)

    for dz, kind in ((1, 0), (3, 1)):
        arrive("w", dz, kind)
        send(("w on", kind), weights.at[SLOT[NZ - dz, 0], kind], weights.at[SLOT[FAR], kind], along_z[dz])
    for dx, part in ((1, 0), (3, 1)):
        arrive("feat", dx, part)
        source = feat.at[pl.ds((NX - dx) * tok + part * half, half)]
        send(("feat on", part), source, feat.at[pl.ds(2 * tok + part * half, half)], along_x[dx])
    for kind in (0, 1):
        arrive("w", "y", kind)
        for dz in (1, 3):
            source = weights.at[SLOT[OWN_MATE], kind]
            send(("w mate", dz, kind), source, weights.at[SLOT[NZ - dz, 1], kind], along_z[dz])

    for number, ((dz, dy), part) in enumerate(pieces):
        for dx in (1, 3, 2):
            source = turned[part].at[index_of(dx, dy, dz)]
            plan(("cot", dx, number), source, cots[part].at[NX - dx - 1, SLOT[dz, dy]], along_x[dx])
    for slot, part in pieces:
        dz, dy = slot
        if slot == FAR_MATE:
            plan(("far", part), terms[part].at[SLOT[slot]], far[part], across)
        elif slot == FAR:
            plan(("relay", part), terms[part].at[SLOT[slot]], relay[part], along_z[relayed(part)])
        elif slot in (NEXT_MATE, BACK_MATE):
            plan(("term", dz, dy, part), terms[part].at[SLOT[slot]], sums[part].at[dz // 2, dy], along_z[dz])
        for kind in (0, 1):
            if slot == OWN_MATE:
                plan(("cross", part, kind), terms[part].at[SLOT[slot], kind], crossed[part].at[kind], across)
            elif slot == OWN:
                plan(("swap", part, kind), stepped[part].at[kind], other[part].at[kind], mate)
            elif slot in (NEXT, BACK):
                there = sums[part].at[dz // 2, dy, kind]
                plan(("term", dz, dy, part, kind), terms[part].at[SLOT[slot], kind], there, along_z[dz])

    def send_cots(number):
        if number < len(pieces):
            for dx in (1, 3, 2):
                go("cot", dx, number)

    for number in range(AHEAD):
        send_cots(number)
    for kind in (0, 1):
        arrive("w on", kind)
        send(("w far", kind), weights.at[SLOT[FAR], kind], weights.at[SLOT[FAR_MATE], kind], across)
    for item in local:
        item.wait()
    arrive("feat", 1, 1)
    arrive("feat", 3, 0)
    arrive("feat on", 0)
    arrive("feat on", 1)

    def products(part, slot, own):
        n = size[part]
        both = [weights[slot, kind, span[part]].astype(F32) for kind in (0, 1)]
        both = jnp.concatenate(both, 0).astype(BF16)
        made = lax.dot_general(both, feat[...], (((1,), (1,)), ((), ())), preferred_element_type=F32) * factor
        gate, upward = made[:n], made[n:]
        blocks = [turned[part][own]] + [cots[part][dx, slot] for dx in range(NX - 1)]
        tangent = jnp.concatenate([block.astype(F32) for block in blocks], 1)
        sigma = jax.nn.sigmoid(gate)
        scaled = factor * tangent * sigma
        diffs = [scaled * upward * (1.0 + gate * (1.0 - sigma)), scaled * gate]
        diffs = jnp.concatenate(diffs, 0).astype(BF16)
        grad[pl.ds(0, 2 * n)] = jnp.dot(diffs, feat[...], preferred_element_type=F32)

    def finish(part):
        n = size[part]
        for kind, out in ((0, mom_gate), (1, mom_up)):
            arrive("term", 1, 0, part, kind)
            arrive("term", 3, 0, part, kind)
            arrive("cross", part, kind)
            value = grad[pl.ds(kind * n, n)] + crossed[part][kind].astype(F32)
            value = value + sums[part][0, 0, kind].astype(F32) + sums[part][1, 0, kind].astype(F32)
            moment = (MOMENT_DECAY * moments[kind, span[part]].astype(F32) + value).astype(BF16)
            out[span[part]] = moment
            weight = weights[SLOT[OWN], kind, span[part]].astype(F32)
            stepped[part][kind] = (weight - STEP_RATE * moment.astype(F32)).astype(BF16)
            go("swap", part, kind)

    slots = [SLOT[slot] for slot, part in pieces]
    owns = [index_of(0, dy, dz) for (dz, dy), part in pieces]

    def work(index, carry):
        for number, (slot, part) in enumerate(pieces):

            @pl.when(index == number)
            def _():
                dz, dy = slot
                for name in {
                    FAR_MATE: (("w far", 0), ("w far", 1)),
                    NEXT_MATE: (("w mate", 3, 0), ("w mate", 3, 1)),
                    BACK_MATE: (("w mate", 1, 0), ("w mate", 1, 1)),
                    NEXT: (("w", 3, 0),),
                    BACK: (("w", 1, 1),),
                }.get(slot, ()):
                    arrive(*name)
                for dx in (1, 3, 2):
                    arrive("cot", dx, number)
                send_cots(number + AHEAD)

        slot_here, own_here = choose(slots, index), choose(owns, index)
        part_here = choose([part for slot, part in pieces], index)
        for part in range(n_parts):

            @pl.when(part_here == part)
            def _():
                products(part, slot_here, own_here)

        for number, (slot, part) in enumerate(pieces):

            @pl.when(index == number)
            def _():
                dz, dy = slot
                n = size[part]
                if slot == OWN:
                    finish(part)
                    return
                for kind in (0, 1):
                    term = grad[pl.ds(kind * n, n)]
                    if slot == FAR:
                        arrive("far", part)
                        term = term + far[part][kind].astype(F32)
                    elif slot == OWN_MATE:
                        arrive("term", 1, dy, part)
                        arrive("term", 3, dy, part)
                        term = term + sums[part][0, dy, kind].astype(F32) + sums[part][1, dy, kind].astype(F32)
                    elif dy == 0 and dz == relayed(part):
                        arrive("relay", part)
                        term = term + relay[part][kind].astype(F32)
                    terms[part][SLOT[slot], kind] = term.astype(BF16)
                    if slot == OWN_MATE:
                        go("cross", part, kind)
                    elif slot in (NEXT, BACK):
                        go("term", dz, dy, part, kind)
                if slot == FAR_MATE:
                    go("far", part)
                elif slot == FAR:
                    go("relay", part)
                elif slot in (NEXT_MATE, BACK_MATE):
                    go("term", dz, dy, part)

        return carry

    lax.fori_loop(0, len(pieces), work, 0)

    for name, item in sent.items():
        if name[0] != "swap":
            item.wait_send()
    for part in range(n_parts):
        for kind, out in ((0, new_gate), (1, new_up)):
            arrive("swap", part, kind)
            average = (stepped[part][kind].astype(F32) + other[part][kind].astype(F32)) * 0.5
            out[span[part]] = average.astype(BF16)

    for name, item in sent.items():
        if name[0] == "swap":
            item.wait_send()


def step_call(stride, features, cotangent, gate_weight, up_weight, gate_moment, up_moment):
    tok, width = features.shape
    rows = gate_weight.shape[0]
    hidden = cotangent.shape[1]
    slots = hidden // rows
    size = sizes(rows, stride)
    sems = 20 + 36 * len(size)
    dma = pltpu.SemaphoreType.DMA
    out = jax.ShapeDtypeStruct((rows, width), BF16)

    def parts(*lead, last=width):
        return [pltpu.VMEM((*lead, n, last), BF16) for n in size]

    return pl.pallas_call(
        functools.partial(step_kernel, stride),
        out_shape=(out,) * 4,
        in_specs=[pl.BlockSpec(memory_space=pl.ANY)] * 6,
        out_specs=(pl.BlockSpec(memory_space=pltpu.VMEM),) * 4,
        scratch_shapes=[
            pltpu.VMEM((NX * tok, width), BF16),
            pltpu.VMEM((tok, hidden), BF16),
            pltpu.VMEM((NY * NZ, 2, rows, width), BF16),
            pltpu.VMEM((2, rows, width), BF16),
            pltpu.VMEM((2 * max(size), width), F32),
            dma((sems,)),
            dma((sems,)),
            dma((6,)),
            *parts(slots, last=tok),
            *parts(NX - 1, NY * NZ, last=tok),
            *parts(NY * NZ - 1, 2),
            *parts(2),
            *parts(2),
            *parts(2, 2, 2),
            *parts(2),
            *parts(2),
            *parts(2),
        ],
        compiler_params=pltpu.CompilerParams(
            collective_id=stride - 1, has_side_effects=True, vmem_limit_bytes=56 * 2**20
        ),
        cost_estimate=pl.CostEstimate(
            flops=8 * tok * hidden * width, bytes_accessed=2 * tok * (hidden + width), transcendentals=tok * hidden
        ),
        name=f"step_stride_{stride}",
    )(features, cotangent, gate_weight, up_weight, gate_moment, up_moment)


def store_kernel(*refs):
    sources, targets, sem = refs[:4], refs[4:8], refs[8]
    copies = [pltpu.make_async_copy(s, t, sem.at[i]) for i, (s, t) in enumerate(zip(sources, targets))]
    for item in copies:
        item.start()
    for item in copies:
        item.wait()


def store(arrays):
    return pl.pallas_call(
        store_kernel,
        out_shape=tuple(jax.ShapeDtypeStruct(a.shape, a.dtype) for a in arrays),
        in_specs=[pl.BlockSpec(memory_space=pltpu.VMEM)] * 4,
        out_specs=(pl.BlockSpec(memory_space=pl.ANY),) * 4,
        scratch_shapes=[pltpu.SemaphoreType.DMA((4,))],
        name="store",
    )(*arrays)


def body(features, cotangent, gate_weight, up_weight, gate_moment, up_moment, step_index):
    arrays = [a[0] for a in (features, cotangent, gate_weight, up_weight, gate_moment, up_moment)]
    nbits = lax.axis_size("rep").bit_length() - 1
    branches = [functools.partial(step_call, 2**bit) for bit in range(nbits)]
    results = store(lax.switch(lax.rem(step_index, nbits), branches, *arrays))
    return tuple(result[None] for result in results)


def solution(mesh):
    split = P("rep", "fsdp", None)
    return jax.shard_map(
        body, mesh=mesh, in_specs=(split,) * 6 + (P(),), out_specs=(split,) * 4, check_vma=False
    )
```

```python
import functools

import jax
import jax.numpy as jnp
from jax import lax
from jax.experimental import pallas as pl
from jax.experimental.pallas import tpu as pltpu
from jax.sharding import PartitionSpec as P

MESH = pl.DeviceIdType.MESH
F32 = jnp.float32
BF16 = jnp.bfloat16
MOMENT_DECAY = 0.9
STEP_RATE = 0.5

NX, NY, NZ = 4, 2, 4
PLACES = {
    "far": (2, 0),
    "far mate": (2, 1),
    "next": (1, 0),
    "next mate": (1, 1),
    "back": (3, 0),
    "back mate": (3, 1),
    "own": (0, 0),
    "own mate": (0, 1),
}
FAR, FAR_MATE, NEXT, NEXT_MATE, BACK, BACK_MATE, OWN, OWN_MATE = PLACES.values()
SLOT = {place: i for i, place in enumerate((FAR_MATE, NEXT_MATE, BACK_MATE, FAR, OWN_MATE, NEXT, BACK, OWN))}
ORDERS = {
    1: (
        ("next mate", 0), ("back mate", 0), ("far mate", 0), ("back mate", 1), ("next mate", 1), ("far mate", 1), ("far", 0), ("back", 0),
        ("own mate", 0), ("next", 0), ("far", 1), ("own mate", 1), ("next", 1), ("back", 1), ("own", 0), ("own", 1),
    ),
    2: (
        ("next mate", 1), ("far mate", 0), ("back mate", 0), ("next mate", 0), ("far mate", 1), ("far", 0), ("back mate", 1), ("own mate", 0),
        ("back", 0), ("next", 0), ("own mate", 1), ("far", 1), ("own", 0), ("next", 1), ("back", 1), ("own", 1),
    ),
}
ORDERS = {stride: tuple((PLACES[name], part) for name, part in order) for stride, order in ORDERS.items()}
FIRST = {1: 96, 2: 80}
AHEAD = 6


def sizes(rows, stride):
    return FIRST[stride], rows - FIRST[stride]


def choose(values, index):
    result = values[0]
    for number, value in enumerate(values[1:], 1):
        result = jnp.where(index == number, value, result)
    return result


def step_kernel(stride, feat_hbm, cot_hbm, gate_hbm, up_hbm, gmom_hbm, umom_hbm, *refs):
    new_gate, new_up, mom_gate, mom_up = refs[:4]
    (feat, raw, weights, moments, grad, send_sems, recv_sems, local_sem) = refs[4:12]
    n_parts = len(sizes(gate_hbm.shape[0], stride))
    turned, cots, terms, far, relay, sums, crossed, stepped, other = (
        refs[12 + i * n_parts : 12 + (i + 1) * n_parts] for i in range(9)
    )
    pieces = ORDERS[stride]
    tok, width = feat_hbm.shape
    rows = gate_hbm.shape[0]
    size = sizes(rows, stride)
    first = [sum(size[:part]) for part in range(n_parts)]
    span = [pl.ds(first[part], size[part]) for part in range(n_parts)]
    half = tok // 2
    factor = width ** (-0.5)
    rep, place = lax.axis_index("rep"), lax.axis_index("fsdp")
    x, y, z = place // (NY * NZ), lax.rem(place // NZ, NY), lax.rem(place, NZ)

    def index_of(dx, dy, dz):
        return lax.rem(x + dx, NX) * (NY * NZ) + lax.rem(y + dy, NY) * NZ + lax.rem(z + dz, NZ)

    mate = (rep + 1 - 2 * lax.rem(rep, 2), place) if stride == 1 else (lax.rem(rep + 2, 4), place)
    across = (rep, index_of(0, 1, 0))
    along_x = {dx: (rep, index_of(dx, 0, 0)) for dx in (1, 2, 3)}
    along_z = {dz: (rep, index_of(0, 0, dz)) for dz in (1, 3)}
    sent = {}

    def relayed(part):
        return 1 if part % 2 == 0 else 3

    def plan(name, src, dst, target):
        number = len(sent)
        sent[name] = pltpu.make_async_remote_copy(
            src_ref=src,
            dst_ref=dst,
            send_sem=send_sems.at[number],
            recv_sem=recv_sems.at[number],
            device_id=target,
            device_id_type=MESH,
        )

    def go(*name):
        sent[name].start()

    def send(name, src, dst, target):
        plan(name, src, dst, target)
        go(*name)

    arrived = set()

    def arrive(*name):
        if name not in arrived:
            arrived.add(name)
            sent[name].wait_recv()

    barrier = pltpu.get_barrier_semaphore()
    greeted = [mate, across, *along_x.values(), *along_z.values()]
    for target in greeted:
        pl.semaphore_signal(barrier, inc=1, device_id=target, device_id_type=MESH)
    turn_copy = pltpu.make_async_copy(cot_hbm, raw, local_sem.at[0])
    turn_copy.start()
    local = [
        pltpu.make_async_copy(feat_hbm, feat.at[pl.ds(0, tok)], local_sem.at[1]),
        pltpu.make_async_copy(gate_hbm, weights.at[SLOT[OWN], 0], local_sem.at[2]),
        pltpu.make_async_copy(up_hbm, weights.at[SLOT[OWN], 1], local_sem.at[3]),
        pltpu.make_async_copy(gmom_hbm, moments.at[0], local_sem.at[4]),
        pltpu.make_async_copy(umom_hbm, moments.at[1], local_sem.at[5]),
    ]
    for item in local:
        item.start()
    pl.semaphore_wait(barrier, len(greeted))

    own_weights = (gate_hbm, up_hbm)

    def send_features(dx, part):
        there = feat.at[pl.ds((NX - dx) * tok + part * half, half)]
        send(("feat", dx, part), feat_hbm.at[pl.ds(part * half, half)], there, along_x[dx])

    for kind in (0, 1):
        send_features(1, kind)
        send_features(3, 1 - kind)
        for dz, what in ((1, kind), (3, 1 - kind)):
            send(("w", dz, what), own_weights[what], weights.at[SLOT[NZ - dz, 0], what], along_z[dz])
        send(("w", "y", kind), own_weights[kind], weights.at[SLOT[OWN_MATE], kind], across)
    turn_copy.wait()
    group = 16 * rows

    def turn(g, carry):
        flat = raw[:, pl.ds(pl.multiple_of(g * group, 128), group)].astype(F32).T
        for s in range(16):
            for part in range(n_parts):
                top = s * rows + first[part]
                turned[part][g * 16 + s] = flat[top : top + size[part]].astype(BF16)
        return carry

    lax.fori_loop(0, raw.shape[1] // group, turn, 0)

    for dz, kind in ((1, 0), (3, 1)):
        arrive("w", dz, kind)
        send(("w on", kind), weights.at[SLOT[NZ - dz, 0], kind], weights.at[SLOT[FAR], kind], along_z[dz])
    for dx, part in ((1, 0), (3, 1)):
        arrive("feat", dx, part)
        source = feat.at[pl.ds((NX - dx) * tok + part * half, half)]
        send(("feat on", part), source, feat.at[pl.ds(2 * tok + part * half, half)], along_x[dx])
    for kind in (0, 1):
        arrive("w", "y", kind)
        for dz in (1, 3):
            source = weights.at[SLOT[OWN_MATE], kind]
            send(("w mate", dz, kind), source, weights.at[SLOT[NZ - dz, 1], kind], along_z[dz])

    for number, ((dz, dy), part) in enumerate(pieces):
        for dx in (1, 3, 2):
            source = turned[part].at[index_of(dx, dy, dz)]
            plan(("cot", dx, number), source, cots[part].at[NX - dx - 1, SLOT[dz, dy]], along_x[dx])
    for slot, part in pieces:
        dz, dy = slot
        if slot == FAR_MATE:
            plan(("far", part), terms[part].at[SLOT[slot]], far[part], across)
        elif slot == FAR:
            plan(("relay", part), terms[part].at[SLOT[slot]], relay[part], along_z[relayed(part)])
        elif slot in (NEXT_MATE, BACK_MATE):
            plan(("term", dz, dy, part), terms[part].at[SLOT[slot]], sums[part].at[dz // 2, dy], along_z[dz])
        for kind in (0, 1):
            if slot == OWN_MATE:
                plan(("cross", part, kind), terms[part].at[SLOT[slot], kind], crossed[part].at[kind], across)
            elif slot == OWN:
                plan(("swap", part, kind), stepped[part].at[kind], other[part].at[kind], mate)
            elif slot in (NEXT, BACK):
                there = sums[part].at[dz // 2, dy, kind]
                plan(("term", dz, dy, part, kind), terms[part].at[SLOT[slot], kind], there, along_z[dz])

    def send_cots(number):
        if number < len(pieces):
            for dx in (1, 3, 2):
                go("cot", dx, number)

    for number in range(AHEAD):
        send_cots(number)
    for kind in (0, 1):
        arrive("w on", kind)
        send(("w far", kind), weights.at[SLOT[FAR], kind], weights.at[SLOT[FAR_MATE], kind], across)
    for item in local:
        item.wait()
    arrive("feat", 1, 1)
    arrive("feat", 3, 0)
    arrive("feat on", 0)
    arrive("feat on", 1)

    def products(part, slot, own):
        n = size[part]
        both = [weights[slot, kind, span[part]].astype(F32) for kind in (0, 1)]
        both = jnp.concatenate(both, 0).astype(BF16)
        made = lax.dot_general(both, feat[...], (((1,), (1,)), ((), ())), preferred_element_type=F32) * factor
        gate, upward = made[:n], made[n:]
        blocks = [turned[part][own]] + [cots[part][dx, slot] for dx in range(NX - 1)]
        tangent = jnp.concatenate([block.astype(F32) for block in blocks], 1)
        sigma = jax.nn.sigmoid(gate)
        scaled = factor * tangent * sigma
        diffs = [scaled * upward * (1.0 + gate * (1.0 - sigma)), scaled * gate]
        diffs = jnp.concatenate(diffs, 0).astype(BF16)
        grad[pl.ds(0, 2 * n)] = jnp.dot(diffs, feat[...], preferred_element_type=F32)

    def finish(part):
        n = size[part]
        for kind, out in ((0, mom_gate), (1, mom_up)):
            arrive("term", 1, 0, part, kind)
            arrive("term", 3, 0, part, kind)
            arrive("cross", part, kind)
            value = grad[pl.ds(kind * n, n)] + crossed[part][kind].astype(F32)
            value = value + sums[part][0, 0, kind].astype(F32) + sums[part][1, 0, kind].astype(F32)
            moment = (MOMENT_DECAY * moments[kind, span[part]].astype(F32) + value).astype(BF16)
            out[span[part]] = moment
            weight = weights[SLOT[OWN], kind, span[part]].astype(F32)
            stepped[part][kind] = (weight - STEP_RATE * moment.astype(F32)).astype(BF16)
            go("swap", part, kind)

    slots = [SLOT[slot] for slot, part in pieces]
    owns = [index_of(0, dy, dz) for (dz, dy), part in pieces]

    def work(index, carry):
        for number, (slot, part) in enumerate(pieces):

            @pl.when(index == number)
            def _():
                dz, dy = slot
                for name in {
                    FAR_MATE: (("w far", 0), ("w far", 1)),
                    NEXT_MATE: (("w mate", 3, 0), ("w mate", 3, 1)),
                    BACK_MATE: (("w mate", 1, 0), ("w mate", 1, 1)),
                    NEXT: (("w", 3, 0),),
                    BACK: (("w", 1, 1),),
                }.get(slot, ()):
                    arrive(*name)
                for dx in (1, 3, 2):
                    arrive("cot", dx, number)
                send_cots(number + AHEAD)

        slot_here, own_here = choose(slots, index), choose(owns, index)
        part_here = choose([part for slot, part in pieces], index)
        for part in range(n_parts):

            @pl.when(part_here == part)
            def _():
                products(part, slot_here, own_here)

        for number, (slot, part) in enumerate(pieces):

            @pl.when(index == number)
            def _():
                dz, dy = slot
                n = size[part]
                if slot == OWN:
                    finish(part)
                    return
                for kind in (0, 1):
                    term = grad[pl.ds(kind * n, n)]
                    if slot == FAR:
                        arrive("far", part)
                        term = term + far[part][kind].astype(F32)
                    elif slot == OWN_MATE:
                        arrive("term", 1, dy, part)
                        arrive("term", 3, dy, part)
                        term = term + sums[part][0, dy, kind].astype(F32) + sums[part][1, dy, kind].astype(F32)
                    elif dy == 0 and dz == relayed(part):
                        arrive("relay", part)
                        term = term + relay[part][kind].astype(F32)
                    terms[part][SLOT[slot], kind] = term.astype(BF16)
                    if slot == OWN_MATE:
                        go("cross", part, kind)
                    elif slot in (NEXT, BACK):
                        go("term", dz, dy, part, kind)
                if slot == FAR_MATE:
                    go("far", part)
                elif slot == FAR:
                    go("relay", part)
                elif slot in (NEXT_MATE, BACK_MATE):
                    go("term", dz, dy, part)

        return carry

    lax.fori_loop(0, len(pieces), work, 0)

    for name, item in sent.items():
        if name[0] != "swap":
            item.wait_send()
    for part in range(n_parts):
        for kind, out in ((0, new_gate), (1, new_up)):
            arrive("swap", part, kind)
            average = (stepped[part][kind].astype(F32) + other[part][kind].astype(F32)) * 0.5
            out[span[part]] = average.astype(BF16)

    for name, item in sent.items():
        if name[0] == "swap":
            item.wait_send()


def step_call(stride, features, cotangent, gate_weight, up_weight, gate_moment, up_moment):
    tok, width = features.shape
    rows = gate_weight.shape[0]
    hidden = cotangent.shape[1]
    slots = hidden // rows
    size = sizes(rows, stride)
    sems = 20 + 36 * len(size)
    dma = pltpu.SemaphoreType.DMA
    out = jax.ShapeDtypeStruct((rows, width), BF16)

    def parts(*lead, last=width):
        return [pltpu.VMEM((*lead, n, last), BF16) for n in size]

    return pl.pallas_call(
        functools.partial(step_kernel, stride),
        out_shape=(out,) * 4,
        in_specs=[pl.BlockSpec(memory_space=pl.ANY)] * 6,
        out_specs=(pl.BlockSpec(memory_space=pltpu.VMEM),) * 4,
        scratch_shapes=[
            pltpu.VMEM((NX * tok, width), BF16),
            pltpu.VMEM((tok, hidden), BF16),
            pltpu.VMEM((NY * NZ, 2, rows, width), BF16),
            pltpu.VMEM((2, rows, width), BF16),
            pltpu.VMEM((2 * max(size), width), F32),
            dma((sems,)),
            dma((sems,)),
            dma((6,)),
            *parts(slots, last=tok),
            *parts(NX - 1, NY * NZ, last=tok),
            *parts(NY * NZ - 1, 2),
            *parts(2),
            *parts(2),
            *parts(2, 2, 2),
            *parts(2),
            *parts(2),
            *parts(2),
        ],
        compiler_params=pltpu.CompilerParams(
            collective_id=stride - 1, has_side_effects=True, vmem_limit_bytes=56 * 2**20
        ),
        cost_estimate=pl.CostEstimate(
            flops=8 * tok * hidden * width, bytes_accessed=2 * tok * (hidden + width), transcendentals=tok * hidden
        ),
        name=f"step_stride_{stride}",
    )(features, cotangent, gate_weight, up_weight, gate_moment, up_moment)


def store_kernel(*refs):
    sources, targets, sem = refs[:4], refs[4:8], refs[8]
    copies = [pltpu.make_async_copy(s, t, sem.at[i]) for i, (s, t) in enumerate(zip(sources, targets))]
    for item in copies:
        item.start()
    for item in copies:
        item.wait()


def store(arrays):
    return pl.pallas_call(
        store_kernel,
        out_shape=tuple(jax.ShapeDtypeStruct(a.shape, a.dtype) for a in arrays),
        in_specs=[pl.BlockSpec(memory_space=pltpu.VMEM)] * 4,
        out_specs=(pl.BlockSpec(memory_space=pl.ANY),) * 4,
        scratch_shapes=[pltpu.SemaphoreType.DMA((4,))],
        name="store",
    )(*arrays)


def body(features, cotangent, gate_weight, up_weight, gate_moment, up_moment, step_index):
    arrays = [a[0] for a in (features, cotangent, gate_weight, up_weight, gate_moment, up_moment)]
    nbits = lax.axis_size("rep").bit_length() - 1
    branches = [functools.partial(step_call, 2**bit) for bit in range(nbits)]
    results = store(lax.switch(lax.rem(step_index, nbits), branches, *arrays))
    return tuple(result[None] for result in results)


def solution(mesh):
    split = P("rep", "fsdp", None)
    return jax.shard_map(
        body, mesh=mesh, in_specs=(split,) * 6 + (P(),), out_specs=(split,) * 4, check_vma=False
    )
```

```python
import functools

import jax
import jax.numpy as jnp
from jax import lax
from jax.experimental import pallas as pl
from jax.experimental.pallas import tpu as pltpu
from jax.sharding import PartitionSpec as P

MESH = pl.DeviceIdType.MESH
F32 = jnp.float32
BF16 = jnp.bfloat16
MOMENT_DECAY = 0.9
STEP_RATE = 0.5

NX, NY, NZ = 4, 2, 4
PLACES = {
    "far": (2, 0),
    "far mate": (2, 1),
    "next": (1, 0),
    "next mate": (1, 1),
    "back": (3, 0),
    "back mate": (3, 1),
    "own": (0, 0),
    "own mate": (0, 1),
}
FAR, FAR_MATE, NEXT, NEXT_MATE, BACK, BACK_MATE, OWN, OWN_MATE = PLACES.values()
SLOT = {place: i for i, place in enumerate((FAR_MATE, NEXT_MATE, BACK_MATE, FAR, OWN_MATE, NEXT, BACK, OWN))}
ORDERS = {
    1: (
        ("next mate", 0), ("back mate", 0), ("far mate", 0), ("back mate", 1), ("next mate", 1), ("far mate", 1), ("far", 0), ("back", 0),
        ("own mate", 0), ("next", 0), ("far", 1), ("own mate", 1), ("next", 1), ("back", 1), ("own", 0), ("own", 1),
    ),
    2: (
        ("next mate", 1), ("far mate", 0), ("back mate", 0), ("next mate", 0), ("far mate", 1), ("far", 0), ("back mate", 1), ("own mate", 0),
        ("back", 0), ("next", 0), ("own mate", 1), ("far", 1), ("own", 0), ("next", 1), ("back", 1), ("own", 1),
    ),
}
ORDERS = {stride: tuple((PLACES[name], part) for name, part in order) for stride, order in ORDERS.items()}
FIRST = {1: 96, 2: 80}
AHEAD = 6


def sizes(rows, stride):
    return FIRST[stride], rows - FIRST[stride]


def choose(values, index):
    result = values[0]
    for number, value in enumerate(values[1:], 1):
        result = jnp.where(index == number, value, result)
    return result


def step_kernel(stride, feat_hbm, cot_hbm, gate_hbm, up_hbm, gmom_hbm, umom_hbm, *refs):
    new_gate, new_up, mom_gate, mom_up = refs[:4]
    (feat, raw, weights, moments, grad, send_sems, recv_sems, local_sem) = refs[4:12]
    n_parts = len(sizes(gate_hbm.shape[0], stride))
    turned, cots, terms, far, relay, sums, crossed, stepped, other = (
        refs[12 + i * n_parts : 12 + (i + 1) * n_parts] for i in range(9)
    )
    pieces = ORDERS[stride]
    tok, width = feat_hbm.shape
    rows = gate_hbm.shape[0]
    size = sizes(rows, stride)
    first = [sum(size[:part]) for part in range(n_parts)]
    span = [pl.ds(first[part], size[part]) for part in range(n_parts)]
    half = tok // 2
    factor = width ** (-0.5)
    rep, place = lax.axis_index("rep"), lax.axis_index("fsdp")
    x, y, z = place // (NY * NZ), lax.rem(place // NZ, NY), lax.rem(place, NZ)

    def index_of(dx, dy, dz):
        return lax.rem(x + dx, NX) * (NY * NZ) + lax.rem(y + dy, NY) * NZ + lax.rem(z + dz, NZ)

    mate = (rep + 1 - 2 * lax.rem(rep, 2), place) if stride == 1 else (lax.rem(rep + 2, 4), place)
    across = (rep, index_of(0, 1, 0))
    along_x = {dx: (rep, index_of(dx, 0, 0)) for dx in (1, 2, 3)}
    along_z = {dz: (rep, index_of(0, 0, dz)) for dz in (1, 3)}
    sent = {}

    def relayed(part):
        return 1 if part % 2 == 0 else 3

    def plan(name, src, dst, target):
        number = len(sent)
        sent[name] = pltpu.make_async_remote_copy(
            src_ref=src,
            dst_ref=dst,
            send_sem=send_sems.at[number],
            recv_sem=recv_sems.at[number],
            device_id=target,
            device_id_type=MESH,
        )

    def go(*name):
        sent[name].start()

    def send(name, src, dst, target):
        plan(name, src, dst, target)
        go(*name)

    arrived = set()

    def arrive(*name):
        if name not in arrived:
            arrived.add(name)
            sent[name].wait_recv()

    barrier = pltpu.get_barrier_semaphore()
    greeted = [mate, across, *along_x.values(), *along_z.values()]
    for target in greeted:
        pl.semaphore_signal(barrier, inc=1, device_id=target, device_id_type=MESH)
    turn_copy = pltpu.make_async_copy(cot_hbm, raw, local_sem.at[0])
    turn_copy.start()
    local = [
        pltpu.make_async_copy(feat_hbm, feat.at[pl.ds(0, tok)], local_sem.at[1]),
        pltpu.make_async_copy(gate_hbm, weights.at[SLOT[OWN], 0], local_sem.at[2]),
        pltpu.make_async_copy(up_hbm, weights.at[SLOT[OWN], 1], local_sem.at[3]),
        pltpu.make_async_copy(gmom_hbm, moments.at[0], local_sem.at[4]),
        pltpu.make_async_copy(umom_hbm, moments.at[1], local_sem.at[5]),
    ]
    for item in local:
        item.start()
    pl.semaphore_wait(barrier, len(greeted))

    own_weights = (gate_hbm, up_hbm)

    def send_features(dx, part):
        there = feat.at[pl.ds((NX - dx) * tok + part * half, half)]
        send(("feat", dx, part), feat_hbm.at[pl.ds(part * half, half)], there, along_x[dx])

    for kind in (0, 1):
        send_features(1, kind)
        send_features(3, 1 - kind)
        for dz, what in ((1, kind), (3, 1 - kind)):
            send(("w", dz, what), own_weights[what], weights.at[SLOT[NZ - dz, 0], what], along_z[dz])
        send(("w", "y", kind), own_weights[kind], weights.at[SLOT[OWN_MATE], kind], across)
    turn_copy.wait()
    group = 16 * rows

    def turn(g, carry):
        flat = raw[:, pl.ds(pl.multiple_of(g * group, 128), group)].astype(F32).T
        for s in range(16):
            for part in range(n_parts):
                top = s * rows + first[part]
                turned[part][g * 16 + s] = flat[top : top + size[part]].astype(BF16)
        return carry

    lax.fori_loop(0, raw.shape[1] // group, turn, 0)

    for dz, kind in ((1, 0), (3, 1)):
        arrive("w", dz, kind)
        send(("w on", kind), weights.at[SLOT[NZ - dz, 0], kind], weights.at[SLOT[FAR], kind], along_z[dz])
    for dx, part in ((1, 0), (3, 1)):
        arrive("feat", dx, part)
        source = feat.at[pl.ds((NX - dx) * tok + part * half, half)]
        send(("feat on", part), source, feat.at[pl.ds(2 * tok + part * half, half)], along_x[dx])
    for kind in (0, 1):
        arrive("w", "y", kind)
        for dz in (1, 3):
            source = weights.at[SLOT[OWN_MATE], kind]
            send(("w mate", dz, kind), source, weights.at[SLOT[NZ - dz, 1], kind], along_z[dz])

    for number, ((dz, dy), part) in enumerate(pieces):
        for dx in (1, 3, 2):
            source = turned[part].at[index_of(dx, dy, dz)]
            plan(("cot", dx, number), source, cots[part].at[NX - dx - 1, SLOT[dz, dy]], along_x[dx])
    for slot, part in pieces:
        dz, dy = slot
        if slot == FAR_MATE:
            plan(("far", part), terms[part].at[SLOT[slot]], far[part], across)
        elif slot == FAR:
            plan(("relay", part), terms[part].at[SLOT[slot]], relay[part], along_z[relayed(part)])
        elif slot in (NEXT_MATE, BACK_MATE):
            plan(("term", dz, dy, part), terms[part].at[SLOT[slot]], sums[part].at[dz // 2, dy], along_z[dz])
        for kind in (0, 1):
            if slot == OWN_MATE:
                plan(("cross", part, kind), terms[part].at[SLOT[slot], kind], crossed[part].at[kind], across)
            elif slot == OWN:
                plan(("swap", part, kind), stepped[part].at[kind], other[part].at[kind], mate)
            elif slot in (NEXT, BACK):
                there = sums[part].at[dz // 2, dy, kind]
                plan(("term", dz, dy, part, kind), terms[part].at[SLOT[slot], kind], there, along_z[dz])

    def send_cots(number):
        if number < len(pieces):
            for dx in (2, 1, 3):
                go("cot", dx, number)

    for number in range(AHEAD):
        send_cots(number)
    for kind in (0, 1):
        arrive("w on", kind)
        send(("w far", kind), weights.at[SLOT[FAR], kind], weights.at[SLOT[FAR_MATE], kind], across)
    for item in local:
        item.wait()
    arrive("feat", 1, 1)
    arrive("feat", 3, 0)
    arrive("feat on", 0)
    arrive("feat on", 1)

    def products(part, slot, own):
        n = size[part]
        both = [weights[slot, kind, span[part]].astype(F32) for kind in (0, 1)]
        both = jnp.concatenate(both, 0).astype(BF16)
        made = lax.dot_general(both, feat[...], (((1,), (1,)), ((), ())), preferred_element_type=F32) * factor
        gate, upward = made[:n], made[n:]
        blocks = [turned[part][own]] + [cots[part][dx, slot] for dx in range(NX - 1)]
        tangent = jnp.concatenate([block.astype(F32) for block in blocks], 1)
        sigma = jax.nn.sigmoid(gate)
        scaled = factor * tangent * sigma
        diffs = [scaled * upward * (1.0 + gate * (1.0 - sigma)), scaled * gate]
        diffs = jnp.concatenate(diffs, 0).astype(BF16)
        grad[pl.ds(0, 2 * n)] = jnp.dot(diffs, feat[...], preferred_element_type=F32)

    def finish(part):
        n = size[part]
        for kind, out in ((0, mom_gate), (1, mom_up)):
            arrive("term", 1, 0, part, kind)
            arrive("term", 3, 0, part, kind)
            arrive("cross", part, kind)
            value = grad[pl.ds(kind * n, n)] + crossed[part][kind].astype(F32)
            value = value + sums[part][0, 0, kind].astype(F32) + sums[part][1, 0, kind].astype(F32)
            moment = (MOMENT_DECAY * moments[kind, span[part]].astype(F32) + value).astype(BF16)
            out[span[part]] = moment
            weight = weights[SLOT[OWN], kind, span[part]].astype(F32)
            stepped[part][kind] = (weight - STEP_RATE * moment.astype(F32)).astype(BF16)
            go("swap", part, kind)

    slots = [SLOT[slot] for slot, part in pieces]
    owns = [index_of(0, dy, dz) for (dz, dy), part in pieces]

    def work(index, carry):
        for number, (slot, part) in enumerate(pieces):

            @pl.when(index == number)
            def _():
                dz, dy = slot
                for name in {
                    FAR_MATE: (("w far", 0), ("w far", 1)),
                    NEXT_MATE: (("w mate", 3, 0), ("w mate", 3, 1)),
                    BACK_MATE: (("w mate", 1, 0), ("w mate", 1, 1)),
                    NEXT: (("w", 3, 0),),
                    BACK: (("w", 1, 1),),
                }.get(slot, ()):
                    arrive(*name)
                for dx in (1, 3, 2):
                    arrive("cot", dx, number)
                send_cots(number + AHEAD)

        slot_here, own_here = choose(slots, index), choose(owns, index)
        part_here = choose([part for slot, part in pieces], index)
        for part in range(n_parts):

            @pl.when(part_here == part)
            def _():
                products(part, slot_here, own_here)

        for number, (slot, part) in enumerate(pieces):

            @pl.when(index == number)
            def _():
                dz, dy = slot
                n = size[part]
                if slot == OWN:
                    finish(part)
                    return
                for kind in (0, 1):
                    term = grad[pl.ds(kind * n, n)]
                    if slot == FAR:
                        arrive("far", part)
                        term = term + far[part][kind].astype(F32)
                    elif slot == OWN_MATE:
                        arrive("term", 1, dy, part)
                        arrive("term", 3, dy, part)
                        term = term + sums[part][0, dy, kind].astype(F32) + sums[part][1, dy, kind].astype(F32)
                    elif dy == 0 and dz == relayed(part):
                        arrive("relay", part)
                        term = term + relay[part][kind].astype(F32)
                    terms[part][SLOT[slot], kind] = term.astype(BF16)
                    if slot == OWN_MATE:
                        go("cross", part, kind)
                    elif slot in (NEXT, BACK):
                        go("term", dz, dy, part, kind)
                if slot == FAR_MATE:
                    go("far", part)
                elif slot == FAR:
                    go("relay", part)
                elif slot in (NEXT_MATE, BACK_MATE):
                    go("term", dz, dy, part)

        return carry

    lax.fori_loop(0, len(pieces), work, 0)

    for name, item in sent.items():
        if name[0] != "swap":
            item.wait_send()
    for part in range(n_parts):
        for kind, out in ((0, new_gate), (1, new_up)):
            arrive("swap", part, kind)
            average = (stepped[part][kind].astype(F32) + other[part][kind].astype(F32)) * 0.5
            out[span[part]] = average.astype(BF16)

    for name, item in sent.items():
        if name[0] == "swap":
            item.wait_send()


def step_call(stride, features, cotangent, gate_weight, up_weight, gate_moment, up_moment):
    tok, width = features.shape
    rows = gate_weight.shape[0]
    hidden = cotangent.shape[1]
    slots = hidden // rows
    size = sizes(rows, stride)
    sems = 20 + 36 * len(size)
    dma = pltpu.SemaphoreType.DMA
    out = jax.ShapeDtypeStruct((rows, width), BF16)

    def parts(*lead, last=width):
        return [pltpu.VMEM((*lead, n, last), BF16) for n in size]

    return pl.pallas_call(
        functools.partial(step_kernel, stride),
        out_shape=(out,) * 4,
        in_specs=[pl.BlockSpec(memory_space=pl.ANY)] * 6,
        out_specs=(pl.BlockSpec(memory_space=pltpu.VMEM),) * 4,
        scratch_shapes=[
            pltpu.VMEM((NX * tok, width), BF16),
            pltpu.VMEM((tok, hidden), BF16),
            pltpu.VMEM((NY * NZ, 2, rows, width), BF16),
            pltpu.VMEM((2, rows, width), BF16),
            pltpu.VMEM((2 * max(size), width), F32),
            dma((sems,)),
            dma((sems,)),
            dma((6,)),
            *parts(slots, last=tok),
            *parts(NX - 1, NY * NZ, last=tok),
            *parts(NY * NZ - 1, 2),
            *parts(2),
            *parts(2),
            *parts(2, 2, 2),
            *parts(2),
            *parts(2),
            *parts(2),
        ],
        compiler_params=pltpu.CompilerParams(
            collective_id=stride - 1, has_side_effects=True, vmem_limit_bytes=56 * 2**20
        ),
        cost_estimate=pl.CostEstimate(
            flops=8 * tok * hidden * width, bytes_accessed=2 * tok * (hidden + width), transcendentals=tok * hidden
        ),
        name=f"step_stride_{stride}",
    )(features, cotangent, gate_weight, up_weight, gate_moment, up_moment)


def store_kernel(*refs):
    sources, targets, sem = refs[:4], refs[4:8], refs[8]
    copies = [pltpu.make_async_copy(s, t, sem.at[i]) for i, (s, t) in enumerate(zip(sources, targets))]
    for item in copies:
        item.start()
    for item in copies:
        item.wait()


def store(arrays):
    return pl.pallas_call(
        store_kernel,
        out_shape=tuple(jax.ShapeDtypeStruct(a.shape, a.dtype) for a in arrays),
        in_specs=[pl.BlockSpec(memory_space=pltpu.VMEM)] * 4,
        out_specs=(pl.BlockSpec(memory_space=pl.ANY),) * 4,
        scratch_shapes=[pltpu.SemaphoreType.DMA((4,))],
        name="store",
    )(*arrays)


def body(features, cotangent, gate_weight, up_weight, gate_moment, up_moment, step_index):
    arrays = [a[0] for a in (features, cotangent, gate_weight, up_weight, gate_moment, up_moment)]
    nbits = lax.axis_size("rep").bit_length() - 1
    branches = [functools.partial(step_call, 2**bit) for bit in range(nbits)]
    results = store(lax.switch(lax.rem(step_index, nbits), branches, *arrays))
    return tuple(result[None] for result in results)


def solution(mesh):
    split = P("rep", "fsdp", None)
    return jax.shard_map(
        body, mesh=mesh, in_specs=(split,) * 6 + (P(),), out_specs=(split,) * 4, check_vma=False
    )
```
